256 devices in a mesh: row: 16 (over x_lo, y, core), line: 16 (over z, x_hi).
Axes of the slice: x: 4 (x_hi: 2, x_lo: 2; x = x_hi * 2 + x_lo), y: 4, z: 8, core: 2. Of those that a mesh axis runs over, the one named last changes fastest.
Arguments:
- scalar: float32 [16, 768, 3072], P('line', 'row'), may hold values from -6 to 6
- x_velocity: float32 [6, 192, 768], P(None, 'row', 'line'), may hold values from -1 to 1
- y_velocity: float32 [6, 192, 768], P(None, 'row', 'line'), may hold values from -1 to 1
Outputs:
- remeshed: float32 [16, 768, 3072], P('line', 'row')
The draws below stay inside these ranges and needn't reach their ends.
All inputs are finite; a program needn't handle non-finite values.
Results may differ from the reference program's by a relative error of at most 0.0003.
Values sent between devices are 32-bit elements; how exact they have to be, the bound alone decides.
No kernel may reach another device: no remote copies, remote signals or barrier semaphores. Data moves between devices by JAX's collectives and lax.ppermute only.
A program may use at most 128 MiB of HBM per device.

```python
import jax
import jax.numpy as jnp
from jax import lax

NX = 3072
Z = 16
NY = 768
ZV = 6
MX = 768
MY = 192


def levels(stream_key, dims, pieces, least, largest):
    loudness, own = 1.0, jax.random.fold_in(stream_key, 6)
    for dim, blocks in pieces:
        steps = jnp.exp(jax.random.uniform(jax.random.fold_in(own, dim), (blocks,), jnp.float32, least / len(pieces), largest / len(pieces)))
        loudness = loudness * jnp.repeat(steps, dims[dim] // blocks).reshape([-1 if axis == dim else 1 for axis in range(len(dims))])
    return loudness


def normal_values(key, extent, scale, reach, cuts=(), held_as=jnp.bfloat16):
    gain = levels(key, extent, cuts, -0.22, 0.18) if cuts else 1.0
    entries = jax.random.normal(key, extent, jnp.float32) * scale * gain
    return jnp.minimum(jnp.maximum(entries, -reach), reach).astype(held_as)


def setup_inputs(seed: int = 0) -> dict:
    streams_of = jax.random.split(jax.random.key(seed), 4)
    return {
        "scalar": normal_values(streams_of[0], (Z, NY, NX), 1.0, 6.0, ((0, 16), (1, 16)), jnp.float32),
        "x_velocity": jnp.clip(jax.random.uniform(streams_of[1], (ZV, MY, MX), jnp.float32, -1.0, 1.0) * levels(streams_of[1], (ZV, MY, MX), ((1, 16), (2, 16)), -0.4, 0.0), -1.0, 1.0),
        "y_velocity": jnp.clip(jax.random.uniform(streams_of[2], (ZV, MY, MX), jnp.float32, -1.0, 1.0) * levels(streams_of[2], (ZV, MY, MX), ((1, 16), (2, 16)), -0.4, 0.0), -1.0, 1.0),
    }


TIME_STEP = 1.6


def tent_weight(values):
    return jnp.maximum(0.0, 1.0 - jnp.abs(values))


def kernel_m6(values):
    radius = jnp.abs(values)
    inside = -(radius - 1.0) * (25.0 * radius ** 4 - 38.0 * radius ** 3 - 3.0 * radius ** 2 + 12.0 * radius + 12.0) / 12.0
    middle = (radius - 1.0) * (radius - 2.0) * (25.0 * radius ** 3 - 114.0 * radius ** 2 + 153.0 * radius - 48.0) / 24.0
    outside = -(radius - 2.0) * (radius - 3.0) ** 3 * (5.0 * radius - 8.0) / 24.0
    return jnp.where(radius < 1.0, inside, jnp.where(radius < 2.0, middle, jnp.where(radius < 3.0, outside, 0.0)))


def wrap_pad(values, along):
    length_axis = values.shape[along]
    low_side = lax.slice_in_dim(values, length_axis - 3, length_axis, axis=along)
    high_side = lax.slice_in_dim(values, 0, 3, axis=along)
    return jnp.concatenate([low_side, values, high_side], axis=along)


def line_velocity(coarse, displacement, offset, lead_rows, along):
    row_count = displacement.shape[along]
    refined = jnp.repeat(coarse, 4, axis=along)
    shape_list = [1] * displacement.ndim
    shape_list[along] = row_count
    phases = ((jnp.arange(row_count) - lead_rows) % 4).astype(jnp.float32).reshape(shape_list)
    summed = jnp.zeros(displacement.shape, jnp.float32)
    for spread in (-1, 0, 1):
        begin_at = offset + 4 * spread
        picked = lax.slice_in_dim(refined, begin_at, begin_at + row_count, axis=along)
        summed = summed + picked * tent_weight((phases - 1.5 + displacement) / 4.0 - spread)
    return summed


def heun_shift(values, coarse, offset, lead_rows, along):
    resting = line_velocity(coarse, jnp.zeros(values.shape, jnp.float32), offset, lead_rows, along)
    moving = line_velocity(coarse, TIME_STEP * resting, offset, lead_rows, along)
    return 0.5 * TIME_STEP * (resting + moving)


def remesh_periodic(values, displacement, along):
    summed = jnp.zeros(values.shape, jnp.float32)
    for target in range(-4, 5):
        summed = summed + jnp.roll(values * kernel_m6(target - displacement), target, axis=along)
    return summed


def z_weights(planes, coarse_planes):
    fine_index = jnp.arange(planes).astype(jnp.float32)[:, None]
    coarse_index = jnp.arange(coarse_planes).astype(jnp.float32)[None, :]
    return tent_weight((fine_index - 1.5) / 4.0 + 1.0 - coarse_index)


def reference(scalar, x_velocity, y_velocity):
    planes = scalar.shape[0]
    plane_weights = z_weights(planes, x_velocity.shape[0])
    flat_y = line_velocity(wrap_pad(x_velocity, 1), jnp.zeros((x_velocity.shape[0], scalar.shape[1], x_velocity.shape[2]), jnp.float32), 12, 0, 1)
    x_lines = jnp.einsum('kq,qyc->kyc', plane_weights, flat_y, precision=lax.Precision.HIGHEST)
    flat_x = line_velocity(wrap_pad(y_velocity, 2), jnp.zeros((y_velocity.shape[0], y_velocity.shape[1], scalar.shape[2]), jnp.float32), 12, 0, 2)
    y_lines = jnp.einsum('kq,qcx->kcx', plane_weights, flat_x, precision=lax.Precision.HIGHEST)

    def sweep_plane(inputs):
        source, along_x, along_y = inputs
        source = source[None]
        displacement = heun_shift(source, wrap_pad(along_x[None], 2), 12, 0, 2)
        source = remesh_periodic(source, displacement, 2)
        displacement = heun_shift(source, wrap_pad(along_y[None], 1), 12, 0, 1)
        source = remesh_periodic(source, displacement, 1)
        return source[0]

    return lax.map(sweep_plane, (scalar, x_lines, y_lines))
```

```python
import functools

import jax
import jax.numpy as jnp
import numpy as np
from jax import lax
from jax.experimental import pallas as pl
from jax.experimental.pallas import tpu as pltpu
from jax.sharding import PartitionSpec as P

SEGMENTS, LANES, TILE = 24, 128, 8
GROUP = SEGMENTS * TILE
WINDOW = 64


def kernel_parts():
    a = np.polynomial.Polynomial([0.0, 1.0])
    pieces = (
        -(a - 1) * (25 * a**4 - 38 * a**3 - 3 * a**2 + 12 * a + 12) / 12,
        (a - 1) * (a - 2) * (25 * a**3 - 114 * a**2 + 153 * a - 48) / 24,
        -(a - 2) * (a - 3) ** 3 * (5 * a - 8) / 24,
    )
    parts = []
    for middle, piece in zip((0.5, 1.5, 2.5), pieces):
        coefs = piece(middle - a).coef
        parts.append(([float(c) for c in coefs[0::2]], [float(c) for c in coefs[1::2]]))
    return parts


PARTS = kernel_parts()


def products(value, d):
    high = d >= 0.0
    e = d - jnp.where(high, 1.0, -1.0)
    right = e >= 0.0
    t = jnp.abs(e) - 0.5
    tau = t * t
    vt = value * t
    near, far = [], []
    for even, odd in PARTS:
        ev = value * ((even[2] * tau + even[1]) * tau + even[0])
        od = vt * ((odd[2] * tau + odd[1]) * tau + odd[0])
        near.append(ev + od)
        far.append(ev - od)
    q = {0: far[0]}
    q[1] = jnp.where(right, near[0], far[1])
    q[-1] = jnp.where(right, far[1], near[0])
    q[2] = jnp.where(right, near[1], far[2])
    q[-2] = jnp.where(right, far[2], near[1])
    q[3] = jnp.where(right, near[2], 0.0)
    q[-3] = jnp.where(right, 0.0, near[2])
    out = []
    for s in range(-4, 5):
        up, down = q.get(s - 1), q.get(s + 1)
        out.append(jnp.where(high, 0.0 if up is None else up, 0.0 if down is None else down))
    return out


def interp_matrices():
    half = np.zeros((128, 256))
    ident = np.zeros((128, 256))
    plus = np.zeros((128, 256))
    minus = np.zeros((128, 256))
    for fine in range(256):
        c, v = fine // 4 + 32, (fine % 4 - 1.5) / 4
        half[c, fine] += 0.5 * (1 - abs(v))
        half[c + (1 if v > 0 else -1), fine] += 0.5 * abs(v)
        ident[c, fine] = 1
        plus[c + 1, fine], plus[c, fine] = 1, -1
        minus[c, fine], minus[c - 1, fine] = 1, -1
    full = np.concatenate([half, 2 * half + ident, plus, minus], axis=1)
    both = np.concatenate([full, full], axis=0)
    both[0, :256] = (np.arange(256) % 4 - 1.5) / 4
    both[128, :256] = 0
    return both


def row_matrix():
    a = np.zeros((64, 16))
    for row in range(4, 60):
        y = row - 8
        c, v = y // 4 + 2, (y % 4 - 1.5) / 4
        a[row, c] += 1 - abs(v)
        a[row, c + (1 if v > 0 else -1)] += abs(v)
    return np.concatenate([a, a], axis=1)


def z_pair(k):
    at = (k - 1.5) / 4 + 1
    q = int(np.floor(at))
    return q, at - q


def pack_kernel(x_ref, y_ref, out_ref, both):
    both[...] = jnp.zeros_like(both)
    both[:, :, 0:48] = x_ref[...]
    both[:, :, 64:112] = y_ref[...]
    for k in range(16):
        q, w = z_pair(k)
        out_ref[k] = (1 - w) * both[q] + w * both[q + 1]


def pack(x, y):
    return pl.pallas_call(
        pack_kernel,
        out_shape=jax.ShapeDtypeStruct((16, 16, 128), jnp.float32),
        scratch_shapes=[pltpu.VMEM((6, 16, 128), jnp.float32)],
        name="pack_planes",
    )(x, y)


def split(values):
    high = values.astype(jnp.bfloat16)
    low = (values - high.astype(jnp.float32)).astype(jnp.bfloat16)
    return high, low


def windows(lines, left, first):
    rows = lines.shape[0]
    lane0 = lax.broadcasted_iota(jnp.int32, (rows, 128), 1) == 0
    for m in range(12):
        shift = 32 if m % 2 == 0 else 96
        if m < 2:
            rolled = pltpu.roll(lines, shift, 1)
            if m == 0:
                even = rolled
            else:
                odd = rolled
        source = even if m % 2 == 0 else odd
        at = (64 * m - 32 + shift) % 768
        part = jnp.where(lane0, first, source[:, at : at + 128])
        high, low = split(part)
        left[m * rows : (m + 1) * rows, 0:128] = high
        left[m * rows : (m + 1) * rows, 128:256] = low


def row_start(row):
    return (row // TILE) * GROUP + row % TILE


def sweep_kernel(got, scalar, top, bottom, matrix, rows_matrix, out, gx, gy, left_x, left_y, coefs, ylines, source, moved):
    for j in range(16):
        gx[:, 48 * j : 48 * j + 48] = got[j, :, 0:48]
        gy[:, 48 * j : 48 * j + 48] = got[j, :, 64:112]
    high, low = split(gx[...])
    lines = jnp.dot(rows_matrix[...], jnp.concatenate([high, low], axis=0), preferred_element_type=jnp.float32)
    windows(0.8 * lines, left_x, 1.0)
    windows(1.6 * gy[...], left_y, 0.0)
    for q in range(4):
        res = jnp.dot(left_x[...], matrix[:, 256 * q : 256 * q + 256], preferred_element_type=jnp.float32)
        for m in range(12):
            for h in range(2):
                for t in range(8):
                    at = (t * SEGMENTS + 2 * m + h) * TILE
                    coefs[q, at : at + TILE, :] = res[m * 64 + 8 * t : m * 64 + 8 * t + 8, 128 * h : 128 * h + 128]
    res = jnp.dot(left_y[...], matrix[:, 0:256], preferred_element_type=jnp.float32)
    for m in range(12):
        for h in range(2):
            for t in range(2):
                at = (t * SEGMENTS + 2 * m + h) * TILE
                ylines[at : at + TILE, :] = res[m * 16 + 8 * t : m * 16 + 8 * t + 8, 128 * h : 128 * h + 128]
    source[0:GROUP, :] = top[...]
    source[GROUP : 7 * GROUP, :] = scalar[...]
    source[7 * GROUP :, :] = bottom[...]

    lane = lax.broadcasted_iota(jnp.int32, (SEGMENTS, LANES), 1)

    def x_rows(block, carry):
        for r in range(4):
            row = block * 4 + r
            at = pl.ds(row_start(row), SEGMENTS, stride=TILE)
            v, s, dp, dm = (coefs[q, at, :] for q in range(4))
            d = s + v * jnp.where(v >= 0.0, dp, dm)
            parts = products(source[at, :], d)
            total = parts[4]
            ahead = behind = None
            for s in range(1, 5):
                moved_up = pltpu.roll(parts[4 + s], s, 1)
                over = jnp.where(lane < s, moved_up, 0.0)
                ahead = over if ahead is None else ahead + over
                moved_down = pltpu.roll(parts[4 - s], LANES - s, 1)
                under = jnp.where(lane >= LANES - s, moved_down, 0.0)
                behind = under if behind is None else behind + under
                total = total + (moved_up + moved_down)
            total = total - (ahead + behind)
            total = total + (pltpu.roll(ahead, 1, 0) + pltpu.roll(behind, SEGMENTS - 1, 0))
            moved[row] = total
        return carry

    lax.fori_loop(1, 15, x_rows, 0)

    def y_cell(store, cell, carry):
        below, here, above = (ylines[pl.ds(row_start(cell + k), SEGMENTS, stride=TILE), :] for k in (-1, 0, 1))
        dm, dp = here - below, above - here
        acc = list(carry) + [None] * 4
        for r in range(4):
            v0 = (r - 1.5) / 4
            u0 = here + v0 * (dp if v0 > 0 else dm)
            v = v0 + 0.5 * u0
            d = (u0 + here) + v * jnp.where(v >= 0.0, dp, dm)
            parts = products(moved[cell * 4 + r], d)
            for s in range(9):
                acc[r + s] = parts[s] if acc[r + s] is None else acc[r + s] + parts[s]
        if store:
            for r in range(4):
                row = 4 * (cell - 2) + r - 4
                out[pl.ds(row_start(row), SEGMENTS, stride=TILE), :] = acc[r]
        return tuple(acc[4:])

    zero = jnp.zeros((SEGMENTS, LANES), jnp.float32)
    carry = lax.fori_loop(1, 3, functools.partial(y_cell, False), (zero,) * 8)
    lax.fori_loop(3, 15, functools.partial(y_cell, True), carry)


def sweeps(got, scalar, top, bottom):
    matrix = jnp.asarray(interp_matrices(), jnp.bfloat16)
    rows_matrix = jnp.asarray(row_matrix(), jnp.bfloat16)
    return pl.pallas_call(
        sweep_kernel,
        out_shape=jax.ShapeDtypeStruct((6 * GROUP, LANES), jnp.float32),
        scratch_shapes=[
            pltpu.VMEM((16, 768), jnp.float32),
            pltpu.VMEM((16, 768), jnp.float32),
            pltpu.VMEM((12 * 64, 256), jnp.bfloat16),
            pltpu.VMEM((12 * 16, 256), jnp.bfloat16),
            pltpu.VMEM((4, 8 * GROUP, LANES), jnp.float32),
            pltpu.VMEM((2 * GROUP, LANES), jnp.float32),
            pltpu.VMEM((8 * GROUP, LANES), jnp.float32),
            pltpu.VMEM((64, SEGMENTS, LANES), jnp.float32),
        ],
        compiler_params=pltpu.CompilerParams(vmem_limit_bytes=32 * 2**20),
        name="sweeps",
    )(got, scalar, top, bottom, matrix, rows_matrix)


def local(scalar, x_velocity, y_velocity):
    count = lax.axis_size("row")
    up = [(i, (i + 1) % count) for i in range(count)]
    down = [((i + 1) % count, i) for i in range(count)]
    tiles = scalar.reshape(6, TILE, SEGMENTS, LANES).transpose(0, 2, 1, 3).reshape(6 * GROUP, LANES)
    pair = jnp.stack([x_velocity, y_velocity])
    low = lax.ppermute(pair[:, :, 10:], "row", up)
    high = lax.ppermute(pair[:, :, :2], "row", down)
    pair = jnp.concatenate([low, pair, high], axis=2)
    top = lax.ppermute(tiles[5 * GROUP :], "row", up)
    bottom = lax.ppermute(tiles[:GROUP], "row", down)
    got = lax.all_to_all(pack(pair[0], pair[1]), "line", 0, 0, tiled=True)
    result = sweeps(got, tiles, top, bottom)
    return result.reshape(6, SEGMENTS, TILE, LANES).transpose(0, 2, 1, 3).reshape(1, 48, 3072)


def solution(mesh):
    in_specs = (P("line", "row", None), P(None, "row", "line"), P(None, "row", "line"))
    out_specs = P("line", "row", None)
    return jax.shard_map(local, mesh=mesh, in_specs=in_specs, out_specs=out_specs, check_vma=False)
```

```python
import functools

import jax
import jax.numpy as jnp
import numpy as np
from jax import lax
from jax.experimental import pallas as pl
from jax.experimental.pallas import tpu as pltpu
from jax.sharding import PartitionSpec as P

SEGMENTS, LANES, TILE = 24, 128, 8
GROUP = SEGMENTS * TILE
WINDOW = 64


def kernel_parts():
    a = np.polynomial.Polynomial([0.0, 1.0])
    pieces = (
        -(a - 1) * (25 * a**4 - 38 * a**3 - 3 * a**2 + 12 * a + 12) / 12,
        (a - 1) * (a - 2) * (25 * a**3 - 114 * a**2 + 153 * a - 48) / 24,
        -(a - 2) * (a - 3) ** 3 * (5 * a - 8) / 24,
    )
    parts = []
    for middle, piece in zip((0.5, 1.5, 2.5), pieces):
        coefs = piece(middle - a).coef
        parts.append(([float(c) for c in coefs[0::2]], [float(c) for c in coefs[1::2]]))
    return parts


PARTS = kernel_parts()


def products(value, d):
    high = d >= 0.0
    e = d - jnp.where(high, 1.0, -1.0)
    right = e >= 0.0
    t = jnp.abs(e) - 0.5
    tau = t * t
    vt = value * t
    near, far = [], []
    for even, odd in PARTS:
        ev = value * ((even[2] * tau + even[1]) * tau + even[0])
        od = vt * ((odd[2] * tau + odd[1]) * tau + odd[0])
        near.append(ev + od)
        far.append(ev - od)
    q = {0: far[0]}
    q[1] = jnp.where(right, near[0], far[1])
    q[-1] = jnp.where(right, far[1], near[0])
    q[2] = jnp.where(right, near[1], far[2])
    q[-2] = jnp.where(right, far[2], near[1])
    q[3] = jnp.where(right, near[2], 0.0)
    q[-3] = jnp.where(right, 0.0, near[2])
    out = []
    for s in range(-4, 5):
        up, down = q.get(s - 1), q.get(s + 1)
        out.append(jnp.where(high, 0.0 if up is None else up, 0.0 if down is None else down))
    return out


def interp_matrices():
    half = np.zeros((128, 256))
    ident = np.zeros((128, 256))
    plus = np.zeros((128, 256))
    minus = np.zeros((128, 256))
    for fine in range(256):
        c, v = fine // 4 + 32, (fine % 4 - 1.5) / 4
        half[c, fine] += 0.5 * (1 - abs(v))
        half[c + (1 if v > 0 else -1), fine] += 0.5 * abs(v)
        ident[c, fine] = 1
        plus[c + 1, fine], plus[c, fine] = 1, -1
        minus[c, fine], minus[c - 1, fine] = 1, -1
    full = np.concatenate([half, 2 * half + ident, plus, minus], axis=1)
    both = np.concatenate([full, full], axis=0)
    both[0, :256] = (np.arange(256) % 4 - 1.5) / 4
    both[128, :256] = 0
    return both


def row_matrix(fine_rows, coarse_rows):
    a = np.zeros((len(fine_rows), len(coarse_rows)))
    for i, y in enumerate(fine_rows):
        c, v = y // 4, (y % 4 - 1.5) / 4
        for cell, weight in ((c, 1 - abs(v)), (c + (1 if v > 0 else -1), abs(v))):
            if cell in coarse_rows:
                a[i, coarse_rows.index(cell)] += weight
    return np.concatenate([a, a], axis=1)


INNER_ROWS, INNER_CELLS = list(range(48)), list(range(16))
EDGE_ROWS = list(range(-4, 4)) + list(range(44, 52))
EDGE_CELLS = [-2, -1, 0, 1, 10, 11, 12, 13]


def z_pair(k):
    at = (k - 1.5) / 4 + 1
    q = int(np.floor(at))
    return q, at - q


def pack_kernel(x_ref, y_ref, out_ref, both):
    both[...] = jnp.zeros_like(both)
    both[:, 0:12, 0:48] = x_ref[...]
    both[:, 0:12, 64:112] = y_ref[...]
    for k in range(16):
        q, w = z_pair(k)
        out_ref[k] = (1 - w) * both[q] + w * both[q + 1]


def pack(x, y):
    return pl.pallas_call(
        pack_kernel,
        out_shape=jax.ShapeDtypeStruct((16, 16, 128), jnp.float32),
        scratch_shapes=[pltpu.VMEM((6, 16, 128), jnp.float32)],
        name="pack_planes",
    )(x, y)


def split(values):
    high = values.astype(jnp.bfloat16)
    low = (values - high.astype(jnp.float32)).astype(jnp.bfloat16)
    return high, low


def windows(lines, left, first):
    rows = lines.shape[0]
    lane0 = lax.broadcasted_iota(jnp.int32, (rows, 128), 1) == 0
    for m in range(12):
        shift = 32 if m % 2 == 0 else 96
        if m < 2:
            rolled = pltpu.roll(lines, shift, 1)
            if m == 0:
                even = rolled
            else:
                odd = rolled
        source = even if m % 2 == 0 else odd
        at = (64 * m - 32 + shift) % 768
        part = jnp.where(lane0, first, source[:, at : at + 128])
        high, low = split(part)
        left[m * rows : (m + 1) * rows, 0:128] = high
        left[m * rows : (m + 1) * rows, 128:256] = low


def row_start(row):
    return (row // TILE) * GROUP + row % TILE


def spread(left, matrix, columns, rows, store):
    res = jnp.dot(left, matrix[:, columns], preferred_element_type=jnp.float32)
    for m in range(12):
        for h in range(2):
            for t in range(rows // TILE):
                at = m * rows + t * TILE
                store(t, 2 * m + h, res[at : at + TILE, LANES * h : LANES * h + LANES])


def fine_fields(gx, gy, left_x, left_y, coefs, ylines, matrix, rows_matrix):
    high, low = split(gx)
    lines = jnp.dot(rows_matrix[...], jnp.concatenate([high, low], axis=0), preferred_element_type=jnp.float32)
    windows(0.8 * lines, left_x, 1.0)
    windows(1.6 * gy, left_y, 0.0)
    for q in range(4):

        def store(t, seg, values):
            coefs[q, pl.ds((t * SEGMENTS + seg) * TILE, TILE), :] = values

        spread(left_x[...], matrix, slice(256 * q, 256 * q + 256), lines.shape[0], store)

    def store_y(t, seg, values):
        if t < ylines.shape[0] // GROUP:
            ylines[pl.ds((t * SEGMENTS + seg) * TILE, TILE), :] = values

    spread(left_y[...], matrix, slice(0, 256), gy.shape[0], store_y)


def row_at(row):
    return pl.ds((row // TILE) * GROUP + row % TILE, SEGMENTS, stride=TILE)


def x_swept(coefs, at, value, lane):
    v, s, dp, dm = (coefs[q, at, :] for q in range(4))
    parts = products(value, s + v * jnp.where(v >= 0.0, dp, dm))
    total = parts[4]
    ahead = behind = None
    for s in range(1, 5):
        raised = pltpu.roll(parts[4 + s], s, 1)
        over = jnp.where(lane < s, raised, 0.0)
        ahead = over if ahead is None else ahead + over
        lowered = pltpu.roll(parts[4 - s], LANES - s, 1)
        under = jnp.where(lane >= LANES - s, lowered, 0.0)
        behind = under if behind is None else behind + under
        total = total + (raised + lowered)
    total = total - (ahead + behind)
    return total + (pltpu.roll(ahead, 1, 0) + pltpu.roll(behind, SEGMENTS - 1, 0))


def y_products(ylines, cell, source):
    below, here, above = (ylines[row_at(cell + k), :] for k in (-1, 0, 1))
    dm, dp = here - below, above - here
    for r in range(4):
        v0 = (r - 1.5) / 4
        u0 = here + v0 * (dp if v0 > 0 else dm)
        v = v0 + 0.5 * u0
        yield products(source(r), (u0 + here) + v * jnp.where(v >= 0.0, dp, dm))


def lanes():
    return lax.broadcasted_iota(jnp.int32, (SEGMENTS, LANES), 1)


def inner_kernel(got, scalar, matrix, rows_matrix, out, partial, gx, gy, left_x, left_y, coefs, ylines, moved, done, sems):
    for j in range(16):
        gx[:, 48 * j : 48 * j + 48] = got[j, :, 0:48]
        gy[:, 48 * j : 48 * j + 48] = got[j, :, 64:112]
    fine_fields(gx[...], gy[...], left_x, left_y, coefs, ylines, matrix, rows_matrix)
    lane = lanes()

    def x_rows(block, carry):
        for r in range(4):
            row = block * 4 + r
            at = row_at(row)
            moved[row] = x_swept(coefs, at, scalar[at, :], lane)
        return carry

    lax.fori_loop(0, 12, x_rows, 0)

    def y_cell(cell, carry):
        acc = list(carry) + [None] * 4
        for r, parts in enumerate(y_products(ylines, cell, lambda r: moved[cell * 4 + r])):
            for s in range(9):
                acc[r + s] = parts[s] if acc[r + s] is None else acc[r + s] + parts[s]
        return acc

    zero = jnp.zeros((SEGMENTS, LANES), jnp.float32)

    def first_cell(cell, carry):
        acc = y_cell(cell, carry)
        for r in range(4):
            partial[4 * (cell - 1) + r] = acc[r]
        return tuple(acc[4:])

    carry = lax.fori_loop(1, 3, first_cell, (zero,) * 8)

    def tile_copy(tile):
        at = pl.ds(tile * GROUP, GROUP)
        return pltpu.make_async_copy(done.at[at, :], out.at[at, :], sems.at[tile])

    for tile in range(1, 5):

        def cell_rows(cell, carry):
            acc = y_cell(cell, carry)
            for r in range(4):
                done[row_at(4 * cell - 4 + r), :] = acc[r]
            return tuple(acc[4:])

        carry = lax.fori_loop(2 * tile + 1, 2 * tile + 3, cell_rows, carry)
        tile_copy(tile).start()
    for r in range(8):
        partial[8 + r] = carry[r]
    for tile in range(1, 5):
        tile_copy(tile).wait()


def edge_kernel(got, below, above, scalar, top, bottom, partial, matrix, rows_matrix, inner, out, gx, gy, left_x, left_y, coefs, ylines, moved, done, sems):
    del inner
    gy[8:16, :] = jnp.zeros((8, 768), jnp.float32)
    for j in range(16):
        at = slice(48 * j, 48 * j + 48)
        for row, ref in ((0, below[j]), (2, got[j, 0:2, :]), (4, got[j, 10:12, :]), (6, above[j])):
            gx[row : row + 2, at] = ref[:, 0:48]
            gy[row : row + 2, at] = ref[:, 64:112]
    fine_fields(gx[...], gy[...], left_x, left_y, coefs, ylines, matrix, rows_matrix)
    lane = lanes()
    sources = [(top, 4), (scalar, 0), (scalar, 44), (bottom, 0)]
    for i in range(16):
        ref, first = sources[i // 4]
        moved[i] = x_swept(coefs, row_at(i), ref[row_at(first + i % 4), :], lane)
    for side, (cells, tile) in enumerate((((-1, 0), 0), ((11, 12), 5))):
        acc = {8 * tile + r: partial[8 * side + r] for r in range(8)}
        for k, c in enumerate(cells):
            for r, parts in enumerate(y_products(ylines, EDGE_CELLS.index(c), lambda r: moved[8 * side + 4 * k + r])):
                for s in range(9):
                    row = 4 * c + r + s - 4
                    if row in acc:
                        acc[row] = acc[row] + parts[s]
        for r in range(8):
            done[row_at(8 * side + r), :] = acc[8 * tile + r]
        pltpu.make_async_copy(
            done.at[pl.ds(side * GROUP, GROUP), :], out.at[pl.ds(tile * GROUP, GROUP), :], sems.at[side]
        ).start()
    for side, tile in ((0, 0), (1, 5)):
        pltpu.make_async_copy(
            done.at[pl.ds(side * GROUP, GROUP), :], out.at[pl.ds(tile * GROUP, GROUP), :], sems.at[side]
        ).wait()


def scratch(rows, cells, ytiles, done_tiles):
    return [
        pltpu.VMEM((cells, 768), jnp.float32),
        pltpu.VMEM((16, 768), jnp.float32),
        pltpu.VMEM((12 * rows, 256), jnp.bfloat16),
        pltpu.VMEM((12 * 16, 256), jnp.bfloat16),
        pltpu.VMEM((4, rows // TILE * GROUP, LANES), jnp.float32),
        pltpu.VMEM((ytiles * GROUP, LANES), jnp.float32),
        pltpu.VMEM((rows, SEGMENTS, LANES), jnp.float32),
        pltpu.VMEM((done_tiles * GROUP, LANES), jnp.float32),
    ]


VMEM_SPEC = pl.BlockSpec(memory_space=pltpu.VMEM)
ANY_SPEC = pl.BlockSpec(memory_space=pl.ANY)
PARAMS = pltpu.CompilerParams(vmem_limit_bytes=32 * 2**20)


def inner_sweeps(got, scalar, matrix):
    return pl.pallas_call(
        inner_kernel,
        out_shape=(
            jax.ShapeDtypeStruct((6 * GROUP, LANES), jnp.float32),
            jax.ShapeDtypeStruct((16, SEGMENTS, LANES), jnp.float32),
        ),
        in_specs=[VMEM_SPEC] * 4,
        out_specs=(ANY_SPEC, VMEM_SPEC),
        scratch_shapes=scratch(48, 16, 2, 6) + [pltpu.SemaphoreType.DMA((6,))],
        compiler_params=PARAMS,
        cost_estimate=pl.CostEstimate(flops=4 * 10**7, bytes_accessed=16 * 2**20, transcendentals=0),
        name="inner_sweeps",
    )(got, scalar, matrix, jnp.asarray(row_matrix(INNER_ROWS, INNER_CELLS), jnp.bfloat16))


def edge_sweeps(got, below, above, scalar, top, bottom, partial, matrix, inner):
    return pl.pallas_call(
        edge_kernel,
        out_shape=jax.ShapeDtypeStruct((6 * GROUP, LANES), jnp.float32),
        in_specs=[VMEM_SPEC] * 9 + [ANY_SPEC],
        out_specs=ANY_SPEC,
        scratch_shapes=scratch(16, 8, 1, 2) + [pltpu.SemaphoreType.DMA((2,))],
        input_output_aliases={9: 0},
        compiler_params=PARAMS,
        name="edge_sweeps",
    )(got, below, above, scalar, top, bottom, partial, matrix, jnp.asarray(row_matrix(EDGE_ROWS, EDGE_CELLS), jnp.bfloat16), inner)


def local(scalar, x_velocity, y_velocity):
    count = lax.axis_size("row")
    up = [(i, (i + 1) % count) for i in range(count)]
    down = [((i + 1) % count, i) for i in range(count)]
    tiles = scalar.reshape(6, TILE, SEGMENTS, LANES).transpose(0, 2, 1, 3).reshape(6 * GROUP, LANES)
    matrix = jnp.asarray(interp_matrices(), jnp.bfloat16)
    top = lax.ppermute(tiles[5 * GROUP :], "row", up)
    bottom = lax.ppermute(tiles[:GROUP], "row", down)
    got = lax.all_to_all(pack(x_velocity, y_velocity), "line", 0, 0, tiled=True)
    below = lax.ppermute(got[:, 10:12], "row", up)
    above = lax.ppermute(got[:, 0:2], "row", down)
    inner, partial = inner_sweeps(got, tiles, matrix)
    result = edge_sweeps(got, below, above, tiles, top, bottom, partial, matrix, inner)
    return result.reshape(6, SEGMENTS, TILE, LANES).transpose(0, 2, 1, 3).reshape(1, 48, 3072)


def solution(mesh):
    in_specs = (P("line", "row", None), P(None, "row", "line"), P(None, "row", "line"))
    out_specs = P("line", "row", None)
    return jax.shard_map(local, mesh=mesh, in_specs=in_specs, out_specs=out_specs, check_vma=False)
```

```python
import functools

import jax
import jax.numpy as jnp
import numpy as np
from jax import lax
from jax.experimental import pallas as pl
from jax.experimental.pallas import tpu as pltpu
from jax.sharding import PartitionSpec as P

SEGMENTS, LANES, TILE = 24, 128, 8
GROUP = SEGMENTS * TILE
WINDOW = 64


def kernel_parts():
    a = np.polynomial.Polynomial([0.0, 1.0])
    pieces = (
        -(a - 1) * (25 * a**4 - 38 * a**3 - 3 * a**2 + 12 * a + 12) / 12,
        (a - 1) * (a - 2) * (25 * a**3 - 114 * a**2 + 153 * a - 48) / 24,
        -(a - 2) * (a - 3) ** 3 * (5 * a - 8) / 24,
    )
    parts = []
    for middle, piece in zip((0.5, 1.5, 2.5), pieces):
        coefs = piece(middle - a).coef
        parts.append(([float(c) for c in coefs[0::2]], [float(c) for c in coefs[1::2]]))
    return parts


PARTS = kernel_parts()


def products(value, d):
    high = d >= 0.0
    e = d - jnp.where(high, 1.0, -1.0)
    right = e >= 0.0
    t = jnp.abs(e) - 0.5
    tau = t * t
    vt = value * t
    evens, odds = [None], [None]
    for even, odd in PARTS[1:]:
        evens.append(value * ((even[2] * tau + even[1]) * tau + even[0]))
        odds.append(vt * ((odd[2] * tau + odd[1]) * tau + odd[0]))
    evens[0] = 0.5 * value - (evens[1] + evens[2])
    odds[0] = vt - (3.0 * odds[1] + 5.0 * odds[2])
    near = [ev + od for ev, od in zip(evens, odds)]
    far = [ev - od for ev, od in zip(evens, odds)]
    q = {0: far[0]}
    q[1] = jnp.where(right, near[0], far[1])
    q[-1] = jnp.where(right, far[1], near[0])
    q[2] = jnp.where(right, near[1], far[2])
    q[-2] = jnp.where(right, far[2], near[1])
    q[3] = jnp.where(right, near[2], 0.0)
    q[-3] = jnp.where(right, 0.0, near[2])
    out = []
    for s in range(-4, 5):
        up, down = q.get(s - 1), q.get(s + 1)
        out.append(jnp.where(high, 0.0 if up is None else up, 0.0 if down is None else down))
    return out


def fill_matrix(out):
    row = lax.broadcasted_iota(jnp.int32, (128, 256), 0)
    fine = lax.broadcasted_iota(jnp.int32, (128, 256), 1)
    offset = row - 32 - (fine >> 2)
    v = ((fine & 3).astype(jnp.float32) - 1.5) * 0.25
    size = jnp.abs(v)
    own = jnp.where(offset == 0, 1.0, 0.0)
    next_cell = jnp.where(offset == 1, 1.0, 0.0)
    last_cell = jnp.where(offset == -1, 1.0, 0.0)
    value = own * (1.0 - size) + jnp.where(v > 0, next_cell, last_cell) * size
    low = 0.5 * value
    blocks = (jnp.where(row == 0, v, low), value + own, next_cell - own, own - last_cell)
    for q, block in enumerate(blocks):
        block = block.astype(jnp.bfloat16)
        out[0:128, 256 * q : 256 * q + 256] = block
        out[128:256, 256 * q : 256 * q + 256] = block if q else low.astype(jnp.bfloat16)


def row_matrix(fine_rows, coarse_rows):
    a = np.zeros((len(fine_rows), len(coarse_rows)))
    for i, y in enumerate(fine_rows):
        c, v = y // 4, (y % 4 - 1.5) / 4
        for cell, weight in ((c, 1 - abs(v)), (c + (1 if v > 0 else -1), abs(v))):
            if cell in coarse_rows:
                a[i, coarse_rows.index(cell)] += weight
    return np.concatenate([a, a], axis=1)


INNER_ROWS, INNER_CELLS = list(range(48)), list(range(12)) + [None] * 4
EDGE_ROWS = list(range(-4, 4)) + list(range(44, 52))
EDGE_CELLS = [-2, -1, 0, 1, 10, 11, 12, 13] + [None] * 8


def pack_kernel(x_ref, y_ref, out_ref, both):
    both[...] = jnp.zeros_like(both)
    both[:, :, 0:48] = x_ref[...]
    both[:, :, 64:112] = y_ref[...]
    for k in range(16):
        q, w = (k + 2) // 4, ((k + 2) % 4 + 0.5) / 4
        out_ref[k] = (1 - w) * both[q] + w * both[q + 1]


def pack(x, y):
    return pl.pallas_call(
        pack_kernel,
        out_shape=jax.ShapeDtypeStruct((16, 12, 128), jnp.float32),
        scratch_shapes=[pltpu.VMEM((6, 12, 128), jnp.float32)],
        name="pack_planes",
    )(x, y)


def split(values):
    high = values.astype(jnp.bfloat16)
    low = (values - high.astype(jnp.float32)).astype(jnp.bfloat16)
    return high, low


def windows(lines, left, first):
    rows = lines.shape[0]
    lane0 = lax.broadcasted_iota(jnp.int32, (rows, 128), 1) == 0
    for m in range(12):
        shift = 32 if m % 2 == 0 else 96
        if m < 2:
            rolled = pltpu.roll(lines, shift, 1)
            if m == 0:
                even = rolled
            else:
                odd = rolled
        source = even if m % 2 == 0 else odd
        at = (64 * m - 32 + shift) % 768
        part = jnp.where(lane0, first, source[:, at : at + 128])
        high, low = split(part)
        left[m * rows : (m + 1) * rows, 0:128] = high
        left[m * rows : (m + 1) * rows, 128:256] = low


def row_start(row):
    return (row // TILE) * GROUP + row % TILE


def spread(left, matrix, columns, rows, store):
    res = jnp.dot(left, matrix[:, columns], preferred_element_type=jnp.float32)
    for m in range(12):
        for h in range(2):
            for t in range(rows // TILE):
                at = m * rows + t * TILE
                store(t, 2 * m + h, res[at : at + TILE, LANES * h : LANES * h + LANES])


def fine_fields(gx, gy, left_x, left_y, coefs, ylines, matrix, rows_matrix):
    high, low = split(gx)
    lines = jnp.dot(rows_matrix[...], jnp.concatenate([high, low], axis=0), preferred_element_type=jnp.float32)
    windows(0.8 * lines, left_x, 1.0)
    windows(1.6 * gy, left_y, 0.0)
    for q in range(4):

        def store(t, seg, values):
            coefs[q, pl.ds((t * SEGMENTS + seg) * TILE, TILE), :] = values

        spread(left_x[...], matrix, slice(256 * q, 256 * q + 256), lines.shape[0], store)

    def store_y(t, seg, values):
        if t < ylines.shape[0] // GROUP:
            ylines[pl.ds((t * SEGMENTS + seg) * TILE, TILE), :] = values

    spread(left_y[...], matrix, slice(0, 256), gy.shape[0], store_y)


def row_at(row):
    return pl.ds((row // TILE) * GROUP + row % TILE, SEGMENTS, stride=TILE)


def x_swept(coefs, at, value, lane):
    v, s, dp, dm = (coefs[q, at, :] for q in range(4))
    parts = products(value, s + v * jnp.where(v >= 0.0, dp, dm))
    total, wrap = parts[4], None
    for s in range(1, 5):
        raised = pltpu.roll(parts[4 + s], s, 1)
        lowered = pltpu.roll(parts[4 - s], LANES - s, 1)
        over = jnp.where(lane < s, raised, jnp.where(lane >= LANES - s, lowered, 0.0))
        wrap = over if wrap is None else wrap + over
        total = total + (raised + lowered)
    moved_wrap = jnp.where(lane < LANES // 2, pltpu.roll(wrap, 1, 0), pltpu.roll(wrap, SEGMENTS - 1, 0))
    return (total - wrap) + moved_wrap


def y_products(ylines, cell, source):
    below, here, above = (ylines[row_at(cell + k), :] for k in (-1, 0, 1))
    dm, dp = here - below, above - here
    for r in range(4):
        v0 = (r - 1.5) / 4
        u0 = here + v0 * (dp if v0 > 0 else dm)
        v = v0 + 0.5 * u0
        yield products(source(r), (u0 + here) + v * jnp.where(v >= 0.0, dp, dm))


def lanes():
    return lax.broadcasted_iota(jnp.int32, (SEGMENTS, LANES), 1)


KEPT = (2, 3, 44, 45)


def inner_kernel(got, scalar, rows_matrix, done, partial, kept, matrix, gx, gy, left_x, left_y, coefs, ylines, moved):
    gx[8:16, :] = jnp.zeros((8, 768), jnp.float32)
    gy[8:16, :] = jnp.zeros((8, 768), jnp.float32)
    for j in range(16):
        gx[0:12, 48 * j : 48 * j + 48] = got[j, :, 0:48]
        gy[0:12, 48 * j : 48 * j + 48] = got[j, :, 64:112]
    fill_matrix(matrix)
    fine_fields(gx[...], gy[...], left_x, left_y, coefs, ylines, matrix, rows_matrix[0:48, :])
    lane = lanes()

    def x_rows(block, carry):
        for r in range(22):
            row = block * 22 + r + 2
            at = row_at(row)
            moved[row] = x_swept(coefs, at, scalar[at, :], lane)
        return carry

    lax.fori_loop(0, 2, x_rows, 0)
    for i, row in enumerate(KEPT):
        kept[i] = moved[row]

    def y_cell(cell, acc):
        acc = acc + [None] * 4
        for r, parts in enumerate(y_products(ylines, cell, lambda r: moved[cell * 4 + r])):
            for s in range(9):
                acc[r + s] = parts[s] if acc[r + s] is None else acc[r + s] + parts[s]
        return acc

    acc = [None] * 8
    for cell in (1, 2):
        acc = y_cell(cell, acc)
        for r in range(4):
            partial[4 * (cell - 1) + r] = acc[r]
        acc = acc[4:]

    for cell in range(3, 11):
        acc = y_cell(cell, acc)
        for r in range(4):
            done[row_at(4 * cell - 12 + r), :] = acc[r]
        acc = acc[4:]
    for r in range(8):
        partial[8 + r] = acc[r]


def edge_kernel(odd_ref, got, line_a, line_b, scalar, tile_a, tile_b, partial, kept, matrix, done, rows_matrix, out, gx, gy, left_x, left_y, coefs, ylines, moved, edge, sems):
    inner_copy = pltpu.make_async_copy(done, out.at[pl.ds(GROUP, 4 * GROUP), :], sems.at[2])
    inner_copy.start()
    gx[8:16, :] = jnp.zeros((8, 768), jnp.float32)
    odd = odd_ref[0] == 1
    gy[8:16, :] = jnp.zeros((8, 768), jnp.float32)
    for j in range(16):
        at = slice(48 * j, 48 * j + 48)
        from_a, from_b = line_a[j], line_b[j]
        below, above = jnp.where(odd, from_a, from_b), jnp.where(odd, from_b, from_a)
        for row, values in ((0, below), (2, got[j, 0:2, :]), (4, got[j, 10:12, :]), (6, above)):
            gx[row : row + 2, at] = values[:, 0:48]
            gy[row : row + 2, at] = values[:, 64:112]
    fine_fields(gx[...], gy[...], left_x, left_y, coefs, ylines, matrix, rows_matrix[48:64, :])
    lane = lanes()
    for i, y in enumerate(EDGE_ROWS):
        if y in KEPT:
            moved[i] = kept[KEPT.index(y)]
            continue
        if 0 <= y < 48:
            value = scalar[row_at(y), :]
        else:
            at = row_at(y % TILE)
            from_a, from_b = tile_a[at, :], tile_b[at, :]
            value = jnp.where(odd, from_a, from_b) if y < 0 else jnp.where(odd, from_b, from_a)
        moved[i] = x_swept(coefs, row_at(i), value, lane)

    def tile_copy(side, tile):
        return pltpu.make_async_copy(
            edge.at[pl.ds(side * GROUP, GROUP), :], out.at[pl.ds(tile * GROUP, GROUP), :], sems.at[side]
        )

    for side, (cells, tile) in enumerate((((-1, 0), 0), ((11, 12), 5))):
        acc = {8 * tile + r: partial[8 * side + r] for r in range(8)}
        for k, c in enumerate(cells):
            for r, parts in enumerate(y_products(ylines, EDGE_CELLS.index(c), lambda r: moved[8 * side + 4 * k + r])):
                for s in range(9):
                    row = 4 * c + r + s - 4
                    if row in acc:
                        acc[row] = acc[row] + parts[s]
        for r in range(8):
            edge[row_at(8 * side + r), :] = acc[8 * tile + r]
        tile_copy(side, tile).start()
    inner_copy.wait()
    tile_copy(0, 0).wait()
    tile_copy(1, 5).wait()


def scratch(rows, ytiles):
    return [
        pltpu.VMEM((16, 768), jnp.float32),
        pltpu.VMEM((16, 768), jnp.float32),
        pltpu.VMEM((12 * rows, 256), jnp.bfloat16),
        pltpu.VMEM((12 * 16, 256), jnp.bfloat16),
        pltpu.VMEM((4, rows // TILE * GROUP, LANES), jnp.float32),
        pltpu.VMEM((ytiles * GROUP, LANES), jnp.float32),
        pltpu.VMEM((rows, SEGMENTS, LANES), jnp.float32),
    ]


VMEM_SPEC = pl.BlockSpec(memory_space=pltpu.VMEM)
ANY_SPEC = pl.BlockSpec(memory_space=pl.ANY)
PARAMS = pltpu.CompilerParams(vmem_limit_bytes=32 * 2**20)


def rows_matrices():
    return jnp.asarray(
        np.concatenate([row_matrix(INNER_ROWS, INNER_CELLS), row_matrix(EDGE_ROWS, EDGE_CELLS)]), jnp.bfloat16
    )


def inner_sweeps(got, scalar, rows_matrix):
    return pl.pallas_call(
        inner_kernel,
        out_shape=(
            jax.ShapeDtypeStruct((4 * GROUP, LANES), jnp.float32),
            jax.ShapeDtypeStruct((16, SEGMENTS, LANES), jnp.float32),
            jax.ShapeDtypeStruct((4, SEGMENTS, LANES), jnp.float32),
            jax.ShapeDtypeStruct((256, 1024), jnp.bfloat16),
        ),
        in_specs=[VMEM_SPEC] * 3,
        out_specs=(VMEM_SPEC,) * 4,
        scratch_shapes=scratch(48, 2),
        compiler_params=PARAMS,
        cost_estimate=pl.CostEstimate(flops=4 * 10**7, bytes_accessed=16 * 2**20, transcendentals=0),
        name="inner_sweeps",
    )(got, scalar, rows_matrix)


def edge_sweeps(odd, got, line_a, line_b, scalar, tile_a, tile_b, partial, kept, matrix, done, rows_matrix):
    return pl.pallas_call(
        edge_kernel,
        out_shape=jax.ShapeDtypeStruct((6 * GROUP, LANES), jnp.float32),
        in_specs=[pl.BlockSpec(memory_space=pltpu.SMEM)] + [VMEM_SPEC] * 11,
        out_specs=ANY_SPEC,
        scratch_shapes=scratch(16, 1)
        + [pltpu.VMEM((2 * GROUP, LANES), jnp.float32), pltpu.SemaphoreType.DMA((3,))],
        compiler_params=PARAMS,
        name="edge_sweeps",
    )(odd, got, line_a, line_b, scalar, tile_a, tile_b, partial, kept, matrix, done, rows_matrix)


def local(scalar, x_velocity, y_velocity):
    count = lax.axis_size("row")
    pair_a = [(i, i ^ 1) for i in range(count)]
    pair_b = [(i, (i + (1 if i % 2 else -1)) % count) for i in range(count)]
    odd = lax.axis_index("row") % 2
    tiles = scalar.reshape(6, TILE, SEGMENTS, LANES).transpose(0, 2, 1, 3).reshape(6 * GROUP, LANES)
    first, last = tiles[:GROUP], tiles[5 * GROUP :]
    tile_a = lax.ppermute(jnp.where(odd == 1, first, last), "row", pair_a)
    tile_b = lax.ppermute(jnp.where(odd == 1, last, first), "row", pair_b)
    packed = pack(x_velocity, y_velocity)
    got = lax.all_to_all(packed, "line", 0, 0, tiled=True)
    first, last = got[:, 0:2], got[:, 10:12]
    line_a = lax.ppermute(jnp.where(odd == 1, first, last), "row", pair_a)
    line_b = lax.ppermute(jnp.where(odd == 1, last, first), "row", pair_b)
    rows_matrix = rows_matrices()
    done, partial, kept, matrix = inner_sweeps(got, tiles, rows_matrix)
    result = edge_sweeps(
        odd.astype(jnp.int32).reshape(1), got, line_a, line_b, tiles, tile_a, tile_b, partial, kept, matrix, done, rows_matrix
    )
    return result.reshape(6, SEGMENTS, TILE, LANES).transpose(0, 2, 1, 3).reshape(1, 48, 3072)


def solution(mesh):
    in_specs = (P("line", "row", None), P(None, "row", "line"), P(None, "row", "line"))
    out_specs = P("line", "row", None)
    return jax.shard_map(local, mesh=mesh, in_specs=in_specs, out_specs=out_specs, check_vma=False)
```

```python
import functools

import jax
import jax.numpy as jnp
import numpy as np
from jax import lax
from jax.experimental import pallas as pl
from jax.experimental.pallas import tpu as pltpu
from jax.sharding import PartitionSpec as P

SEGMENTS, LANES, TILE = 24, 128, 8
GROUP = SEGMENTS * TILE
PITCH = 9
WINDOW = 64


def kernel_parts():
    a = np.polynomial.Polynomial([0.0, 1.0])
    pieces = (
        -(a - 1) * (25 * a**4 - 38 * a**3 - 3 * a**2 + 12 * a + 12) / 12,
        (a - 1) * (a - 2) * (25 * a**3 - 114 * a**2 + 153 * a - 48) / 24,
        -(a - 2) * (a - 3) ** 3 * (5 * a - 8) / 24,
    )
    parts = []
    for middle, piece in zip((0.5, 1.5, 2.5), pieces):
        coefs = piece(middle - a).coef
        parts.append(([float(c) for c in coefs[0::2]], [float(c) for c in coefs[1::2]]))
    return parts


PARTS = kernel_parts()


def products(value, d):
    high = d >= 0.0
    e = d - jnp.where(high, 1.0, -1.0)
    right = e >= 0.0
    t = jnp.abs(e) - 0.5
    tau = t * t
    vt = value * t
    evens, odds = [None], [None]
    for even, odd in PARTS[1:]:
        evens.append(value * ((even[2] * tau + even[1]) * tau + even[0]))
        odds.append(vt * ((odd[2] * tau + odd[1]) * tau + odd[0]))
    evens[0] = 0.5 * value - (evens[1] + evens[2])
    odds[0] = vt - (3.0 * odds[1] + 5.0 * odds[2])
    near = [ev + od for ev, od in zip(evens, odds)]
    far = [ev - od for ev, od in zip(evens, odds)]
    q = {0: far[0]}
    q[1] = jnp.where(right, near[0], far[1])
    q[-1] = jnp.where(right, far[1], near[0])
    q[2] = jnp.where(right, near[1], far[2])
    q[-2] = jnp.where(right, far[2], near[1])
    q[3] = jnp.where(right, near[2], 0.0)
    q[-3] = jnp.where(right, 0.0, near[2])
    out = []
    for s in range(-4, 5):
        up, down = q.get(s - 1), q.get(s + 1)
        out.append(jnp.where(high, 0.0 if up is None else up, 0.0 if down is None else down))
    return out


def fill_matrix(out):
    row = lax.broadcasted_iota(jnp.int32, (128, 256), 0)
    fine = lax.broadcasted_iota(jnp.int32, (128, 256), 1)
    offset = row - 32 - (fine >> 2)
    v = ((fine & 3).astype(jnp.float32) - 1.5) * 0.25
    size = jnp.abs(v)
    own = jnp.where(offset == 0, 1.0, 0.0)
    next_cell = jnp.where(offset == 1, 1.0, 0.0)
    last_cell = jnp.where(offset == -1, 1.0, 0.0)
    value = own * (1.0 - size) + jnp.where(v > 0, next_cell, last_cell) * size
    low = 0.5 * value
    blocks = (jnp.where(row == 0, v, low), value + own, next_cell - own, own - last_cell)
    for q, block in enumerate(blocks):
        block = block.astype(jnp.bfloat16)
        out[0:128, 256 * q : 256 * q + 256] = block
        out[128:256, 256 * q : 256 * q + 256] = block if q else low.astype(jnp.bfloat16)


def row_matrix(fine_rows, coarse_rows):
    a = np.zeros((len(fine_rows), len(coarse_rows)))
    for i, y in enumerate(fine_rows):
        c, v = y // 4, (y % 4 - 1.5) / 4
        for cell, weight in ((c, 1 - abs(v)), (c + (1 if v > 0 else -1), abs(v))):
            if cell in coarse_rows:
                a[i, coarse_rows.index(cell)] += weight
    return np.concatenate([a, a], axis=1)


INNER_ROWS, INNER_CELLS = list(range(48)), list(range(12)) + [None] * 4
EDGE_ROWS = list(range(-4, 4)) + list(range(44, 52))
EDGE_CELLS = [-2, -1, 0, 1, 10, 11, 12, 13] + [None] * 8


def pack_kernel(x_ref, y_ref, out_ref, both):
    both[...] = jnp.zeros_like(both)
    both[:, :, 0:48] = x_ref[...]
    both[:, :, 64:112] = y_ref[...]
    for k in range(16):
        q, w = (k + 2) // 4, ((k + 2) % 4 + 0.5) / 4
        out_ref[k] = (1 - w) * both[q] + w * both[q + 1]


def pack(x, y):
    return pl.pallas_call(
        pack_kernel,
        out_shape=jax.ShapeDtypeStruct((16, 12, 128), jnp.float32),
        scratch_shapes=[pltpu.VMEM((6, 12, 128), jnp.float32)],
        name="pack_planes",
    )(x, y)


def split(values):
    high = values.astype(jnp.bfloat16)
    low = (values - high.astype(jnp.float32)).astype(jnp.bfloat16)
    return high, low


def windows(lines, left, first):
    rows = lines.shape[0]
    lane0 = lax.broadcasted_iota(jnp.int32, (rows, 128), 1) == 0
    for m in range(12):
        shift = 32 if m % 2 == 0 else 96
        if m < 2:
            rolled = pltpu.roll(lines, shift, 1)
            if m == 0:
                even = rolled
            else:
                odd = rolled
        source = even if m % 2 == 0 else odd
        at = (64 * m - 32 + shift) % 768
        part = jnp.where(lane0, first, source[:, at : at + 128])
        high, low = split(part)
        left[m * rows : (m + 1) * rows, 0:128] = high
        left[m * rows : (m + 1) * rows, 128:256] = low


def row_start(row):
    return (row // TILE) * GROUP + row % TILE


def spread(left, matrix, columns, rows, store):
    res = jnp.dot(left, matrix[:, columns], preferred_element_type=jnp.float32)
    for m in range(12):
        for h in range(2):
            for t in range(rows // TILE):
                at = m * rows + t * TILE
                store(t, 2 * m + h, res[at : at + TILE, LANES * h : LANES * h + LANES])


def fine_fields(gx, gy, left_x, left_y, coefs, ylines, matrix, rows_matrix):
    high, low = split(gx)
    lines = jnp.dot(rows_matrix[...], jnp.concatenate([high, low], axis=0), preferred_element_type=jnp.float32)
    windows(0.8 * lines, left_x, 1.0)
    windows(1.6 * gy, left_y, 0.0)
    for q in range(4):

        def store(t, seg, values):
            coefs[q, pl.ds((t * SEGMENTS + seg) * PITCH, TILE), :] = values

        spread(left_x[...], matrix, slice(256 * q, 256 * q + 256), lines.shape[0], store)

    def store_y(t, seg, values):
        if t < ylines.shape[0] // (SEGMENTS * PITCH):
            ylines[pl.ds((t * SEGMENTS + seg) * PITCH, TILE), :] = values

    spread(left_y[...], matrix, slice(0, 256), gy.shape[0], store_y)


def row_at(row):
    return pl.ds((row // TILE) * GROUP + row % TILE, SEGMENTS, stride=TILE)


def field_at(row):
    return pl.ds((row // TILE) * (SEGMENTS * PITCH) + row % TILE, SEGMENTS, stride=PITCH)


def x_swept(coefs, row, value, lane):
    at = field_at(row)
    v, s, dp, dm = (coefs[q, at, :] for q in range(4))
    parts = products(value, s + v * jnp.where(v >= 0.0, dp, dm))
    total, wrap = parts[4], None
    for s in range(1, 5):
        raised = pltpu.roll(parts[4 + s], s, 1)
        lowered = pltpu.roll(parts[4 - s], LANES - s, 1)
        over = jnp.where(lane < s, raised, jnp.where(lane >= LANES - s, lowered, 0.0))
        wrap = over if wrap is None else wrap + over
        total = total + (raised + lowered)
    moved_wrap = jnp.where(lane < LANES // 2, pltpu.roll(wrap, 1, 0), pltpu.roll(wrap, SEGMENTS - 1, 0))
    return (total - wrap) + moved_wrap


def y_products(ylines, cell, source):
    below, here, above = (ylines[field_at(cell + k), :] for k in (-1, 0, 1))
    dm, dp = here - below, above - here
    for r in range(4):
        v0 = (r - 1.5) / 4
        u0 = here + v0 * (dp if v0 > 0 else dm)
        v = v0 + 0.5 * u0
        yield products(source(r), (u0 + here) + v * jnp.where(v >= 0.0, dp, dm))


def lanes():
    return lax.broadcasted_iota(jnp.int32, (SEGMENTS, LANES), 1)


KEPT = (2, 3, 44, 45)


def prepare_kernel(odd_ref, scalar, fine, send_a, send_b, matrix):
    odd = odd_ref[0] == 1
    for y in range(48):
        fine[y] = scalar[row_at(y), :]
    for i in range(4):
        first, last = fine[i], fine[44 + i]
        send_a[i] = jnp.where(odd, first, last)
        send_b[i] = jnp.where(odd, last, first)
    fill_matrix(matrix)


def inner_kernel(got, fine, matrix, rows_matrix, done, partial, kept, gx, gy, left_x, left_y, coefs, ylines, moved):
    gx[8:16, :] = jnp.zeros((8, 768), jnp.float32)
    gy[8:16, :] = jnp.zeros((8, 768), jnp.float32)
    for j in range(16):
        gx[0:12, 48 * j : 48 * j + 48] = got[j, :, 0:48]
        gy[0:12, 48 * j : 48 * j + 48] = got[j, :, 64:112]
    fine_fields(gx[...], gy[...], left_x, left_y, coefs, ylines, matrix, rows_matrix[0:48, :])
    lane = lanes()

    def x_rows(block, carry):
        for r in range(22):
            row = block * 22 + r + 2
            moved[row] = x_swept(coefs, row, fine[row], lane)
        return carry

    lax.fori_loop(0, 2, x_rows, 0)
    for i, row in enumerate(KEPT):
        kept[i] = moved[row]

    def y_cell(cell, acc):
        acc = acc + [None] * 4
        for r, parts in enumerate(y_products(ylines, cell, lambda r: moved[cell * 4 + r])):
            for s in range(9):
                acc[r + s] = parts[s] if acc[r + s] is None else acc[r + s] + parts[s]
        return acc

    acc = [None] * 8
    for cell in (1, 2):
        acc = y_cell(cell, acc)
        for r in range(4):
            partial[4 * (cell - 1) + r] = acc[r]
        acc = acc[4:]

    for cell in range(3, 11):
        acc = y_cell(cell, acc)
        for r in range(4):
            done[row_at(4 * cell - 12 + r), :] = acc[r]
        acc = acc[4:]
    for r in range(8):
        partial[8 + r] = acc[r]


def edge_kernel(odd_ref, got, line_a, line_b, fine, rows_a, rows_b, partial, kept, matrix, done, rows_matrix, out, gx, gy, left_x, left_y, coefs, ylines, moved, edge, sems):
    inner_copy = pltpu.make_async_copy(done, out.at[pl.ds(GROUP, 4 * GROUP), :], sems.at[2])
    inner_copy.start()
    odd = odd_ref[0] == 1
    gx[8:16, :] = jnp.zeros((8, 768), jnp.float32)
    gy[8:16, :] = jnp.zeros((8, 768), jnp.float32)
    for j in range(16):
        at = slice(48 * j, 48 * j + 48)
        from_a, from_b = line_a[j], line_b[j]
        below, above = jnp.where(odd, from_a, from_b), jnp.where(odd, from_b, from_a)
        for row, values in ((0, below), (2, got[j, 0:2, :]), (4, got[j, 10:12, :]), (6, above)):
            gx[row : row + 2, at] = values[:, 0:48]
            gy[row : row + 2, at] = values[:, 64:112]
    fine_fields(gx[...], gy[...], left_x, left_y, coefs, ylines, matrix, rows_matrix[48:64, :])
    lane = lanes()
    for i, y in enumerate(EDGE_ROWS):
        if y in KEPT:
            moved[i] = kept[KEPT.index(y)]
            continue
        if 0 <= y < 48:
            value = fine[y]
        else:
            from_a, from_b = rows_a[y % 4], rows_b[y % 4]
            value = jnp.where(odd, from_a, from_b) if y < 0 else jnp.where(odd, from_b, from_a)
        moved[i] = x_swept(coefs, i, value, lane)

    acc = {row: partial[i] for i, row in enumerate(list(range(8)) + list(range(40, 48)))}
    for k in range(2):
        sides = [
            (8 * side + 4 * k, c, y_products(ylines, EDGE_CELLS.index(c), lambda r, at=8 * side + 4 * k: moved[at + r]))
            for side, c in ((0, k - 1), (1, k + 11))
        ]
        for r in range(4):
            for at, c, values in sides:
                for s, part in enumerate(next(values)):
                    row = 4 * c + r + s - 4
                    if row in acc:
                        acc[row] = acc[row] + part
    copies = []
    for side, tile in ((0, 0), (1, 5)):
        for r in range(8):
            edge[row_at(8 * side + r), :] = acc[8 * tile + r]
        copies.append(
            pltpu.make_async_copy(
                edge.at[pl.ds(side * GROUP, GROUP), :], out.at[pl.ds(tile * GROUP, GROUP), :], sems.at[side]
            )
        )
        copies[-1].start()
    for copy in [inner_copy] + copies:
        copy.wait()


def scratch(rows, ytiles):
    return [
        pltpu.VMEM((16, 768), jnp.float32),
        pltpu.VMEM((16, 768), jnp.float32),
        pltpu.VMEM((12 * rows, 256), jnp.bfloat16),
        pltpu.VMEM((12 * 16, 256), jnp.bfloat16),
        pltpu.VMEM((4, rows // TILE * SEGMENTS * PITCH, LANES), jnp.float32),
        pltpu.VMEM((ytiles * SEGMENTS * PITCH, LANES), jnp.float32),
        pltpu.VMEM((rows, SEGMENTS, LANES), jnp.float32),
    ]


VMEM_SPEC = pl.BlockSpec(memory_space=pltpu.VMEM)
ANY_SPEC = pl.BlockSpec(memory_space=pl.ANY)
PARAMS = pltpu.CompilerParams(vmem_limit_bytes=32 * 2**20)


def rows_matrices():
    return jnp.asarray(
        np.concatenate([row_matrix(INNER_ROWS, INNER_CELLS), row_matrix(EDGE_ROWS, EDGE_CELLS)]), jnp.bfloat16
    )


def prepare(odd, scalar):
    rows = jax.ShapeDtypeStruct((4, SEGMENTS, LANES), jnp.float32)
    return pl.pallas_call(
        prepare_kernel,
        out_shape=(
            jax.ShapeDtypeStruct((48, SEGMENTS, LANES), jnp.float32),
            rows,
            rows,
            jax.ShapeDtypeStruct((256, 1024), jnp.bfloat16),
        ),
        in_specs=[pl.BlockSpec(memory_space=pltpu.SMEM), VMEM_SPEC],
        out_specs=(VMEM_SPEC,) * 4,
        compiler_params=PARAMS,
        name="prepare",
    )(odd, scalar)


def inner_sweeps(got, fine, matrix, rows_matrix):
    return pl.pallas_call(
        inner_kernel,
        out_shape=(
            jax.ShapeDtypeStruct((4 * GROUP, LANES), jnp.float32),
            jax.ShapeDtypeStruct((16, SEGMENTS, LANES), jnp.float32),
            jax.ShapeDtypeStruct((4, SEGMENTS, LANES), jnp.float32),
        ),
        in_specs=[VMEM_SPEC] * 4,
        out_specs=(VMEM_SPEC,) * 3,
        scratch_shapes=scratch(48, 2),
        compiler_params=PARAMS,
        cost_estimate=pl.CostEstimate(flops=4 * 10**7, bytes_accessed=16 * 2**20, transcendentals=0),
        name="inner_sweeps",
    )(got, fine, matrix, rows_matrix)


def edge_sweeps(odd, got, line_a, line_b, fine, rows_a, rows_b, partial, kept, matrix, done, rows_matrix):
    return pl.pallas_call(
        edge_kernel,
        out_shape=jax.ShapeDtypeStruct((6 * GROUP, LANES), jnp.float32),
        in_specs=[pl.BlockSpec(memory_space=pltpu.SMEM)] + [VMEM_SPEC] * 11,
        out_specs=ANY_SPEC,
        scratch_shapes=scratch(16, 1)
        + [pltpu.VMEM((2 * GROUP, LANES), jnp.float32), pltpu.SemaphoreType.DMA((3,))],
        compiler_params=PARAMS,
        name="edge_sweeps",
    )(odd, got, line_a, line_b, fine, rows_a, rows_b, partial, kept, matrix, done, rows_matrix)


def local(scalar, x_velocity, y_velocity):
    count = lax.axis_size("row")
    pair_a = [(i, i ^ 1) for i in range(count)]
    pair_b = [(i, (i + (1 if i % 2 else -1)) % count) for i in range(count)]
    odd = lax.axis_index("row") % 2
    tiles = scalar.reshape(6, TILE, SEGMENTS, LANES).transpose(0, 2, 1, 3).reshape(6 * GROUP, LANES)
    parity = odd.astype(jnp.int32).reshape(1)
    got = lax.all_to_all(pack(x_velocity, y_velocity), "line", 0, 0, tiled=True)
    fine, send_a, send_b, matrix = prepare(parity, tiles)
    rows_a = lax.ppermute(send_a, "row", pair_a)
    rows_b = lax.ppermute(send_b, "row", pair_b)
    first, last = got[:, 0:2], got[:, 10:12]
    line_a = lax.ppermute(jnp.where(odd == 1, first, last), "row", pair_a)
    line_b = lax.ppermute(jnp.where(odd == 1, last, first), "row", pair_b)
    rows_matrix = rows_matrices()
    done, partial, kept = inner_sweeps(got, fine, matrix, rows_matrix)
    result = edge_sweeps(
        parity, got, line_a, line_b, fine, rows_a, rows_b, partial, kept, matrix, done, rows_matrix
    )
    return result.reshape(6, SEGMENTS, TILE, LANES).transpose(0, 2, 1, 3).reshape(1, 48, 3072)


def solution(mesh):
    in_specs = (P("line", "row", None), P(None, "row", "line"), P(None, "row", "line"))
    out_specs = P("line", "row", None)
    return jax.shard_map(local, mesh=mesh, in_specs=in_specs, out_specs=out_specs, check_vma=False)
```

```python
import functools

import jax
import jax.numpy as jnp
import numpy as np
from jax import lax
from jax.experimental import pallas as pl
from jax.experimental.pallas import tpu as pltpu
from jax.sharding import PartitionSpec as P

SEGMENTS, LANES, TILE = 24, 128, 8
GROUP = SEGMENTS * TILE
PITCH = 9
WINDOW = 64


def kernel_parts():
    a = np.polynomial.Polynomial([0.0, 1.0])
    pieces = (
        (1.5, (a - 1) * (a - 2) * (25 * a**3 - 114 * a**2 + 153 * a - 48) / 24),
        (2.5, -(a - 2) * (a - 3) ** 3 * (5 * a - 8) / 24),
    )
    parts = []
    for middle, piece in pieces:
        coefs = piece(middle - a).coef
        for part in (coefs[0::2], coefs[1::2]):
            quotient, rest = divmod(np.polynomial.Polynomial(part), np.polynomial.Polynomial([-0.25, 1.0]))
            assert np.abs(rest.coef).max() < 1e-12
            parts.append([float(c) for c in quotient.coef])
    return parts


PARTS = kernel_parts()


def products(value, d):
    high = d >= 0.0
    size = jnp.abs(d)
    right = size >= 1.0
    t = jnp.abs(size - 1.0) - 0.5
    tau = t * t
    common = value * (tau - 0.25)
    common_t = common * t
    even1, odd1, even2, odd2 = (
        base * (line[1] * tau + line[0]) for base, line in zip((common, common_t) * 2, PARTS)
    )
    even0 = 0.5 * value - (even1 + even2)
    odd0 = value * t - (3.0 * odd1 + 5.0 * odd2)
    far0 = even0 - odd0
    near0 = even0 + odd0
    near1, far1 = even1 + odd1, even1 - odd1
    near2, far2 = even2 + odd2, even2 - odd2
    w = {
        1: far0,
        2: jnp.where(right, near0, far1),
        0: jnp.where(right, far1, near0),
        3: jnp.where(right, near1, far2),
        -1: jnp.where(right, far2, near1),
        4: jnp.where(right, near2, 0.0),
        -2: jnp.where(right, 0.0, near2),
    }
    return [w[0] if s == 0 else jnp.where(high, w.get(s, 0.0), w.get(-s, 0.0)) for s in range(-4, 5)]


def fill_matrix(out):
    row = lax.broadcasted_iota(jnp.int32, (128, 256), 0)
    fine = lax.broadcasted_iota(jnp.int32, (128, 256), 1)
    offset = row - 32 - (fine >> 2)
    v = ((fine & 3).astype(jnp.float32) - 1.5) * 0.25
    size = jnp.abs(v)
    own = jnp.where(offset == 0, 1.0, 0.0)
    next_cell = jnp.where(offset == 1, 1.0, 0.0)
    last_cell = jnp.where(offset == -1, 1.0, 0.0)
    value = own * (1.0 - size) + jnp.where(v > 0, next_cell, last_cell) * size
    low = 0.5 * value
    blocks = (jnp.where(row == 0, v, low), value + own, next_cell - own, own - last_cell)
    for q, block in enumerate(blocks):
        block = block.astype(jnp.bfloat16)
        out[0:128, 256 * q : 256 * q + 256] = block
        out[128:256, 256 * q : 256 * q + 256] = block if q else low.astype(jnp.bfloat16)


def row_matrix(fine_rows, coarse_rows):
    a = np.zeros((len(fine_rows), len(coarse_rows)))
    for i, y in enumerate(fine_rows):
        c, v = y // 4, (y % 4 - 1.5) / 4
        for cell, weight in ((c, 1 - abs(v)), (c + (1 if v > 0 else -1), abs(v))):
            if cell in coarse_rows:
                a[i, coarse_rows.index(cell)] += weight
    return np.concatenate([a, a], axis=1)


INNER_ROWS, INNER_CELLS = list(range(48)), list(range(12)) + [None] * 4
EDGE_ROWS = list(range(-4, 4)) + list(range(44, 52))
EDGE_CELLS = [-2, -1, 0, 1, 10, 11, 12, 13] + [None] * 8


def pack_kernel(x_ref, y_ref, out_ref, both):
    both[...] = jnp.zeros_like(both)
    both[:, :, 0:48] = x_ref[...]
    both[:, :, 64:112] = y_ref[...]
    for k in range(16):
        q, w = (k + 2) // 4, ((k + 2) % 4 + 0.5) / 4
        out_ref[k] = (1 - w) * both[q] + w * both[q + 1]


def pack(x, y):
    return pl.pallas_call(
        pack_kernel,
        out_shape=jax.ShapeDtypeStruct((16, 12, 128), jnp.float32),
        scratch_shapes=[pltpu.VMEM((6, 12, 128), jnp.float32)],
        name="pack_planes",
    )(x, y)


def split(values):
    high = values.astype(jnp.bfloat16)
    low = (values - high.astype(jnp.float32)).astype(jnp.bfloat16)
    return high, low


def windows(lines, left, first):
    rows = lines.shape[0]
    lane0 = lax.broadcasted_iota(jnp.int32, (rows, 128), 1) == 0
    for m in range(12):
        shift = 32 if m % 2 == 0 else 96
        if m < 2:
            rolled = pltpu.roll(lines, shift, 1)
            if m == 0:
                even = rolled
            else:
                odd = rolled
        source = even if m % 2 == 0 else odd
        at = (64 * m - 32 + shift) % 768
        part = jnp.where(lane0, first, source[:, at : at + 128])
        high, low = split(part)
        left[m * rows : (m + 1) * rows, 0:128] = high
        left[m * rows : (m + 1) * rows, 128:256] = low


def row_start(row):
    return (row // TILE) * GROUP + row % TILE


def spread(left, matrix, columns, rows, store):
    res = jnp.dot(left, matrix[:, columns], preferred_element_type=jnp.float32)
    for m in range(12):
        for h in range(2):
            for t in range(rows // TILE):
                at = m * rows + t * TILE
                store(t, 2 * m + h, res[at : at + TILE, LANES * h : LANES * h + LANES])


def fine_fields(gx, gy, left_x, left_y, coefs, ylines, matrix, rows_matrix):
    high, low = split(gx)
    lines = jnp.dot(rows_matrix[...], jnp.concatenate([high, low], axis=0), preferred_element_type=jnp.float32)
    windows(0.8 * lines, left_x, 1.0)
    windows(1.6 * gy, left_y, 0.0)
    for q in range(4):

        def store(t, seg, values):
            coefs[q, pl.ds((t * SEGMENTS + seg) * PITCH, TILE), :] = values

        spread(left_x[...], matrix, slice(256 * q, 256 * q + 256), lines.shape[0], store)

    def store_y(t, seg, values):
        if t < ylines.shape[0] // (SEGMENTS * PITCH):
            ylines[pl.ds((t * SEGMENTS + seg) * PITCH, TILE), :] = values

    spread(left_y[...], matrix, slice(0, 256), gy.shape[0], store_y)


def row_at(row):
    return pl.ds((row // TILE) * GROUP + row % TILE, SEGMENTS, stride=TILE)


def field_at(row):
    return pl.ds((row // TILE) * (SEGMENTS * PITCH) + row % TILE, SEGMENTS, stride=PITCH)


def x_swept(coefs, row, value, lane):
    at = field_at(row)
    v, s, dp, dm = (coefs[q, at, :] for q in range(4))
    parts = products(value, s + v * jnp.where(v >= 0.0, dp, dm))
    total, wrap = parts[4], None
    for s in range(1, 5):
        raised = pltpu.roll(parts[4 + s], s, 1)
        lowered = pltpu.roll(parts[4 - s], LANES - s, 1)
        over = jnp.where(lane < s, raised, jnp.where(lane >= LANES - s, lowered, 0.0))
        wrap = over if wrap is None else wrap + over
        total = total + (raised + lowered)
    moved_wrap = jnp.where(lane < LANES // 2, pltpu.roll(wrap, 1, 0), pltpu.roll(wrap, SEGMENTS - 1, 0))
    return (total - wrap) + moved_wrap


def group_at(start, group, pitch):
    return pl.ds(start + group * TILE * pitch, TILE, stride=pitch)


def y_products(ylines, cell, group, source):
    at = (group_at((k // TILE) * (SEGMENTS * PITCH) + k % TILE, group, PITCH) for k in (cell - 1, cell, cell + 1))
    below, here, above = (ylines[rows, :] for rows in at)
    dm, dp = here - below, above - here
    for r in range(4):
        v0 = (r - 1.5) / 4
        u0 = here + v0 * (dp if v0 > 0 else dm)
        v = v0 + 0.5 * u0
        yield products(source(r), (u0 + here) + v * jnp.where(v >= 0.0, dp, dm))


def finished(ref, row, group, values):
    ref[group_at((row // TILE) * GROUP + row % TILE, group, TILE), :] = values


def lanes():
    return lax.broadcasted_iota(jnp.int32, (SEGMENTS, LANES), 1)


KEPT = (2, 3, 44, 45)


def prepare_kernel(odd_ref, scalar, fine, send_a, send_b, matrix):
    odd = odd_ref[0] == 1
    for y in range(48):
        fine[y] = scalar[row_at(y), :]
    for i in range(4):
        first, last = fine[i], fine[44 + i]
        send_a[i] = jnp.where(odd, first, last)
        send_b[i] = jnp.where(odd, last, first)
    fill_matrix(matrix)


def inner_kernel(got, fine, matrix, rows_matrix, done, partial, kept, gx, gy, left_x, left_y, coefs, ylines, moved):
    gx[8:16, :] = jnp.zeros((8, 768), jnp.float32)
    gy[8:16, :] = jnp.zeros((8, 768), jnp.float32)
    for j in range(16):
        gx[0:12, 48 * j : 48 * j + 48] = got[j, :, 0:48]
        gy[0:12, 48 * j : 48 * j + 48] = got[j, :, 64:112]
    fine_fields(gx[...], gy[...], left_x, left_y, coefs, ylines, matrix, rows_matrix[0:48, :])
    lane = lanes()

    def x_rows(block, carry):
        for r in range(22):
            row = block * 22 + r + 2
            moved[row] = x_swept(coefs, row, fine[row], lane)
        return carry

    lax.fori_loop(0, 2, x_rows, 0)
    for i, row in enumerate(KEPT):
        kept[i] = moved[row]

    for group in range(3):
        segs = slice(TILE * group, TILE * group + TILE)
        acc = [None] * 8
        for cell in range(1, 11):
            acc = acc + [None] * 4
            for r, parts in enumerate(y_products(ylines, cell, group, lambda r: moved[cell * 4 + r, segs, :])):
                for s in range(9):
                    acc[r + s] = parts[s] if acc[r + s] is None else acc[r + s] + parts[s]
            for r in range(4):
                if cell < 3:
                    partial[4 * cell - 4 + r, segs, :] = acc[r]
                else:
                    finished(done, 4 * cell - 12 + r, group, acc[r])
            acc = acc[4:]
        for r in range(8):
            partial[8 + r, segs, :] = acc[r]


def edge_kernel(odd_ref, got, line_a, line_b, fine, rows_a, rows_b, partial, kept, matrix, done, rows_matrix, out, gx, gy, left_x, left_y, coefs, ylines, moved, edge, sems):
    inner_copy = pltpu.make_async_copy(done, out.at[pl.ds(GROUP, 4 * GROUP), :], sems.at[2])
    inner_copy.start()
    odd = odd_ref[0] == 1
    gx[8:16, :] = jnp.zeros((8, 768), jnp.float32)
    gy[8:16, :] = jnp.zeros((8, 768), jnp.float32)
    for j in range(16):
        at = slice(48 * j, 48 * j + 48)
        from_a, from_b = line_a[j], line_b[j]
        below, above = jnp.where(odd, from_a, from_b), jnp.where(odd, from_b, from_a)
        for row, values in ((0, below), (2, got[j, 0:2, :]), (4, got[j, 10:12, :]), (6, above)):
            gx[row : row + 2, at] = values[:, 0:48]
            gy[row : row + 2, at] = values[:, 64:112]
    fine_fields(gx[...], gy[...], left_x, left_y, coefs, ylines, matrix, rows_matrix[48:64, :])
    lane = lanes()
    for i, y in enumerate(EDGE_ROWS):
        if y in KEPT:
            moved[i] = kept[KEPT.index(y)]
            continue
        if 0 <= y < 48:
            value = fine[y]
        else:
            from_a, from_b = rows_a[y % 4], rows_b[y % 4]
            value = jnp.where(odd, from_a, from_b) if y < 0 else jnp.where(odd, from_b, from_a)
        moved[i] = x_swept(coefs, i, value, lane)

    for side, first in ((0, -1), (1, 11)):
        for group in range(3):
            segs = slice(TILE * group, TILE * group + TILE)
            acc = {40 * side + r: partial[8 * side + r, segs, :] for r in range(8)}
            for k in range(2):
                c, at = first + k, 8 * side + 4 * k
                for r, parts in enumerate(y_products(ylines, EDGE_CELLS.index(c), group, lambda r: moved[at + r, segs, :])):
                    for s, part in enumerate(parts):
                        row = 4 * c + r + s - 4
                        if row in acc:
                            acc[row] = acc[row] + part
            for r in range(8):
                finished(edge, 8 * side + r, group, acc[40 * side + r])
    copies = []
    for side, tile in ((0, 0), (1, 5)):
        copies.append(
            pltpu.make_async_copy(
                edge.at[pl.ds(side * GROUP, GROUP), :], out.at[pl.ds(tile * GROUP, GROUP), :], sems.at[side]
            )
        )
        copies[-1].start()
    for copy in [inner_copy] + copies:
        copy.wait()


def scratch(rows, ytiles):
    return [
        pltpu.VMEM((16, 768), jnp.float32),
        pltpu.VMEM((16, 768), jnp.float32),
        pltpu.VMEM((12 * rows, 256), jnp.bfloat16),
        pltpu.VMEM((12 * 16, 256), jnp.bfloat16),
        pltpu.VMEM((4, rows // TILE * SEGMENTS * PITCH, LANES), jnp.float32),
        pltpu.VMEM((ytiles * SEGMENTS * PITCH, LANES), jnp.float32),
        pltpu.VMEM((rows, SEGMENTS, LANES), jnp.float32),
    ]


VMEM_SPEC = pl.BlockSpec(memory_space=pltpu.VMEM)
ANY_SPEC = pl.BlockSpec(memory_space=pl.ANY)
PARAMS = pltpu.CompilerParams(vmem_limit_bytes=32 * 2**20)


def rows_matrices():
    return jnp.asarray(
        np.concatenate([row_matrix(INNER_ROWS, INNER_CELLS), row_matrix(EDGE_ROWS, EDGE_CELLS)]), jnp.bfloat16
    )


def prepare(odd, scalar):
    rows = jax.ShapeDtypeStruct((4, SEGMENTS, LANES), jnp.float32)
    return pl.pallas_call(
        prepare_kernel,
        out_shape=(
            jax.ShapeDtypeStruct((48, SEGMENTS, LANES), jnp.float32),
            rows,
            rows,
            jax.ShapeDtypeStruct((256, 1024), jnp.bfloat16),
        ),
        in_specs=[pl.BlockSpec(memory_space=pltpu.SMEM), VMEM_SPEC],
        out_specs=(VMEM_SPEC,) * 4,
        compiler_params=PARAMS,
        name="prepare",
    )(odd, scalar)


def inner_sweeps(got, fine, matrix, rows_matrix):
    return pl.pallas_call(
        inner_kernel,
        out_shape=(
            jax.ShapeDtypeStruct((4 * GROUP, LANES), jnp.float32),
            jax.ShapeDtypeStruct((16, SEGMENTS, LANES), jnp.float32),
            jax.ShapeDtypeStruct((4, SEGMENTS, LANES), jnp.float32),
        ),
        in_specs=[VMEM_SPEC] * 4,
        out_specs=(VMEM_SPEC,) * 3,
        scratch_shapes=scratch(48, 2),
        compiler_params=PARAMS,
        cost_estimate=pl.CostEstimate(flops=4 * 10**7, bytes_accessed=16 * 2**20, transcendentals=0),
        name="inner_sweeps",
    )(got, fine, matrix, rows_matrix)


def edge_sweeps(odd, got, line_a, line_b, fine, rows_a, rows_b, partial, kept, matrix, done, rows_matrix):
    return pl.pallas_call(
        edge_kernel,
        out_shape=jax.ShapeDtypeStruct((6 * GROUP, LANES), jnp.float32),
        in_specs=[pl.BlockSpec(memory_space=pltpu.SMEM)] + [VMEM_SPEC] * 11,
        out_specs=ANY_SPEC,
        scratch_shapes=scratch(16, 1)
        + [pltpu.VMEM((2 * GROUP, LANES), jnp.float32), pltpu.SemaphoreType.DMA((3,))],
        compiler_params=PARAMS,
        name="edge_sweeps",
    )(odd, got, line_a, line_b, fine, rows_a, rows_b, partial, kept, matrix, done, rows_matrix)


def local(scalar, x_velocity, y_velocity):
    count = lax.axis_size("row")
    pair_a = [(i, i ^ 1) for i in range(count)]
    pair_b = [(i, (i + (1 if i % 2 else -1)) % count) for i in range(count)]
    odd = lax.axis_index("row") % 2
    tiles = scalar.reshape(6, TILE, SEGMENTS, LANES).transpose(0, 2, 1, 3).reshape(6 * GROUP, LANES)
    parity = odd.astype(jnp.int32).reshape(1)
    got = lax.all_to_all(pack(x_velocity, y_velocity), "line", 0, 0, tiled=True)
    fine, send_a, send_b, matrix = prepare(parity, tiles)
    rows_a = lax.ppermute(send_a, "row", pair_a)
    rows_b = lax.ppermute(send_b, "row", pair_b)
    first, last = got[:, 0:2], got[:, 10:12]
    line_a = lax.ppermute(jnp.where(odd == 1, first, last), "row", pair_a)
    line_b = lax.ppermute(jnp.where(odd == 1, last, first), "row", pair_b)
    rows_matrix = rows_matrices()
    done, partial, kept = inner_sweeps(got, fine, matrix, rows_matrix)
    result = edge_sweeps(
        parity, got, line_a, line_b, fine, rows_a, rows_b, partial, kept, matrix, done, rows_matrix
    )
    return result.reshape(6, SEGMENTS, TILE, LANES).transpose(0, 2, 1, 3).reshape(1, 48, 3072)


def solution(mesh):
    in_specs = (P("line", "row", None), P(None, "row", "line"), P(None, "row", "line"))
    out_specs = P("line", "row", None)
    return jax.shard_map(local, mesh=mesh, in_specs=in_specs, out_specs=out_specs, check_vma=False)
```

```python
import functools

import jax
import jax.numpy as jnp
import numpy as np
from jax import lax
from jax.experimental import pallas as pl
from jax.experimental.pallas import tpu as pltpu
from jax.sharding import PartitionSpec as P

SEGMENTS, LANES, TILE = 24, 128, 8
GROUP = SEGMENTS * TILE
PITCH = 9
ORDER = list(range(0, 16, 2)) + list(range(1, 16, 2))


def kernel_parts():
    a = np.polynomial.Polynomial([0.0, 1.0])
    pieces = (
        (1.5, (a - 1) * (a - 2) * (25 * a**3 - 114 * a**2 + 153 * a - 48) / 24),
        (2.5, -(a - 2) * (a - 3) ** 3 * (5 * a - 8) / 24),
    )
    parts = []
    for middle, piece in pieces:
        coefs = piece(middle - a).coef
        for part in (coefs[0::2], coefs[1::2]):
            quotient, rest = divmod(np.polynomial.Polynomial(part), np.polynomial.Polynomial([-0.25, 1.0]))
            assert np.abs(rest.coef).max() < 1e-12
            parts.append([float(c) for c in quotient.coef])
    return parts


PARTS = kernel_parts()


def products(value, d):
    high = d >= 0.0
    size = jnp.abs(d)
    right = size >= 1.0
    t = jnp.abs(size - 1.0) - 0.5
    tau = t * t
    common = value * (tau - 0.25)
    common_t = common * t
    even1, odd1, even2, odd2 = (
        base * (line[1] * tau + line[0]) for base, line in zip((common, common_t) * 2, PARTS)
    )
    even0 = 0.5 * value - (even1 + even2)
    odd0 = value * t - (3.0 * odd1 + 5.0 * odd2)
    far0 = even0 - odd0
    near0 = even0 + odd0
    near1, far1 = even1 + odd1, even1 - odd1
    near2, far2 = even2 + odd2, even2 - odd2
    w = {
        1: far0,
        2: jnp.where(right, near0, far1),
        0: jnp.where(right, far1, near0),
        3: jnp.where(right, near1, far2),
        -1: jnp.where(right, far2, near1),
        4: jnp.where(right, near2, 0.0),
        -2: jnp.where(right, 0.0, near2),
    }
    return [w[0] if s == 0 else jnp.where(high, w.get(s, 0.0), w.get(-s, 0.0)) for s in range(-4, 5)]


def fill_matrix(out):
    row = lax.broadcasted_iota(jnp.int32, (128, 256), 0)
    fine = lax.broadcasted_iota(jnp.int32, (128, 256), 1)
    offset = row - 32 - (fine >> 2)
    v = ((fine & 3).astype(jnp.float32) - 1.5) * 0.25
    size = jnp.abs(v)
    own = jnp.where(offset == 0, 1.0, 0.0)
    next_cell = jnp.where(offset == 1, 1.0, 0.0)
    last_cell = jnp.where(offset == -1, 1.0, 0.0)
    value = own * (1.0 - size) + jnp.where(v > 0, next_cell, last_cell) * size
    low = 0.5 * value
    blocks = (jnp.where(row == 0, v, low), value + own, next_cell - own, own - last_cell)
    for q, block in enumerate(blocks):
        block = block.astype(jnp.bfloat16)
        out[0:128, 256 * q : 256 * q + 256] = block
        out[128:256, 256 * q : 256 * q + 256] = block if q else low.astype(jnp.bfloat16)


def row_matrix(fine_rows, coarse_rows):
    a = np.zeros((len(fine_rows), len(coarse_rows)))
    for i, y in enumerate(fine_rows):
        c, v = y // 4, (y % 4 - 1.5) / 4
        for cell, weight in ((c, 1 - abs(v)), (c + (1 if v > 0 else -1), abs(v))):
            if cell in coarse_rows:
                a[i, coarse_rows.index(cell)] += weight
    return np.concatenate([a, a], axis=1)


INNER_ROWS, INNER_CELLS = list(range(48)), list(range(12)) + [None] * 4
EDGE_ROWS = list(range(-4, 4)) + list(range(44, 52))
EDGE_CELLS = [-2, -1, 0, 1, 10, 11, 12, 13] + [None] * 8


def pack_kernel(x_ref, y_ref, out_ref, both):
    both[...] = jnp.zeros_like(both)
    both[:, :, 0:48] = x_ref[...]
    both[:, :, 64:112] = y_ref[...]
    for i, k in enumerate(ORDER):
        q, w = (k + 2) // 4, ((k + 2) % 4 + 0.5) / 4
        out_ref[i] = (1 - w) * both[q] + w * both[q + 1]


def pack(x, y):
    return pl.pallas_call(
        pack_kernel,
        out_shape=jax.ShapeDtypeStruct((16, 12, 128), jnp.float32),
        scratch_shapes=[pltpu.VMEM((6, 12, 128), jnp.float32)],
        name="pack_planes",
    )(x, y)


def split(values):
    high = values.astype(jnp.bfloat16)
    low = (values - high.astype(jnp.float32)).astype(jnp.bfloat16)
    return high, low


def windows(lines, lefts, first):
    rows = lines.shape[0]
    lane0 = lax.broadcasted_iota(jnp.int32, (rows, 128), 1) == 0
    rolled = [pltpu.roll(lines, shift, 1) for shift in (32, 96)]
    for m in range(12):
        at = (64 * m - 32 + (32, 96)[m % 2]) % 768
        high, low = split(jnp.where(lane0, first, rolled[m % 2][:, at : at + 128]))
        row = 0
        for left in lefts:
            count = left.shape[0] // 12
            for columns, part in ((slice(0, 128), high), (slice(128, 256), low)):
                left[m * count : (m + 1) * count, columns] = part[row : row + count]
            row += count


def spread(left, matrix, columns, rows, store):
    res = jnp.dot(left, matrix[:, columns], preferred_element_type=jnp.float32)
    for m in range(12):
        for h in range(2):
            for t in range(rows // TILE):
                at = m * rows + t * TILE
                store(t, 2 * m + h, res[at : at + TILE, LANES * h : LANES * h + LANES])


def x_lines(gx, rows_matrix):
    high, low = split(gx)
    lines = jnp.dot(rows_matrix[...], jnp.concatenate([high, low], axis=0), preferred_element_type=jnp.float32)
    return 0.8 * lines


def field(left, matrix, q, out):
    def store(t, seg, values):
        if t < out.shape[0] // (SEGMENTS * PITCH):
            out[pl.ds((t * SEGMENTS + seg) * PITCH, TILE), :] = values

    spread(left[...], matrix, slice(256 * q, 256 * q + 256), left.shape[0] // 12, store)


def fine_fields(gx, gy, left_x, left_y, coefs, ylines, matrix, rows_matrix):
    windows(x_lines(gx, rows_matrix), (left_x,), 1.0)
    windows(1.6 * gy, (left_y,), 0.0)
    for q in range(4):
        field(left_x, matrix, q, coefs.at[q])
    field(left_y, matrix, 0, ylines)


def row_at(row):
    return pl.ds((row // TILE) * GROUP + row % TILE, SEGMENTS, stride=TILE)


def field_at(row):
    return pl.ds((row // TILE) * (SEGMENTS * PITCH) + row % TILE, SEGMENTS, stride=PITCH)


def x_swept(coefs, row, value, lane):
    at = field_at(row)
    v, s, dp, dm = (coefs[q, at, :] for q in range(4))
    parts = products(value, s + v * jnp.where(v >= 0.0, dp, dm))
    total, wrap = parts[4], None
    for s in range(1, 5):
        raised = pltpu.roll(parts[4 + s], s, 1)
        lowered = pltpu.roll(parts[4 - s], LANES - s, 1)
        over = jnp.where(lane < s, raised, jnp.where(lane >= LANES - s, lowered, 0.0))
        wrap = over if wrap is None else wrap + over
        total = total + (raised + lowered)
    moved_wrap = jnp.where(lane < LANES // 2, pltpu.roll(wrap, 1, 0), pltpu.roll(wrap, SEGMENTS - 1, 0))
    return (total - wrap) + moved_wrap


def group_at(start, group, pitch):
    return pl.ds(start + group * TILE * pitch, TILE, stride=pitch)


def y_products(ylines, cell, group, source):
    at = (group_at((k // TILE) * (SEGMENTS * PITCH) + k % TILE, group, PITCH) for k in (cell - 1, cell, cell + 1))
    below, here, above = (ylines[rows, :] for rows in at)
    dm, dp = here - below, above - here
    for r in range(4):
        v0 = (r - 1.5) / 4
        u0 = here + v0 * (dp if v0 > 0 else dm)
        v = v0 + 0.5 * u0
        yield products(source(r), (u0 + here) + v * jnp.where(v >= 0.0, dp, dm))


def finished(ref, row, group, values):
    ref[group_at((row // TILE) * GROUP + row % TILE, group, TILE), :] = values


def lanes():
    return lax.broadcasted_iota(jnp.int32, (SEGMENTS, LANES), 1)


KEPT = (2, 3, 44, 45)


def prepare_kernel(odd_ref, scalar, fine, send_a, send_b, matrix):
    odd = odd_ref[0] == 1
    for y in range(48):
        fine[y] = scalar[row_at(y), :]
    for i in range(4):
        first, last = fine[i], fine[44 + i]
        send_a[i] = jnp.where(odd, first, last)
        send_b[i] = jnp.where(odd, last, first)
    fill_matrix(matrix)


def inner_kernel(got, fine, matrix, rows_matrix, done, partial, kept, gx, gy, left_x, left_y, coefs, ylines, moved, left_first, coefs_first):
    gx[8:16, :] = jnp.zeros((8, 768), jnp.float32)
    gy[8:16, :] = jnp.zeros((8, 768), jnp.float32)
    for i, j in enumerate(ORDER):
        gx[0:12, 48 * j : 48 * j + 48] = got[i, :, 0:48]
        gy[0:12, 48 * j : 48 * j + 48] = got[i, :, 64:112]
    windows(x_lines(gx[...], rows_matrix[0:48, :]), (left_first, left_x), 1.0)
    for q in range(4):
        field(left_first, matrix, q, coefs_first.at[q])
    windows(1.6 * gy[...], (left_y,), 0.0)
    lane = lanes()
    for q in range(5):
        field(left_x if q < 4 else left_y, matrix, q % 4, coefs.at[q] if q < 4 else ylines)
        for row in range(2 + 3 * q, min(5 + 3 * q, 16)):
            moved[row] = x_swept(coefs_first, row, fine[row], lane)

    def x_rows(block, carry):
        for r in range(15):
            row = block * 15 + r
            moved[row + 16] = x_swept(coefs, row, fine[row + 16], lane)
        return carry

    lax.fori_loop(0, 2, x_rows, 0)
    for i, row in enumerate(KEPT):
        kept[i] = moved[row]

    for group in range(3):
        segs = slice(TILE * group, TILE * group + TILE)
        acc = [None] * 8
        for cell in range(1, 11):
            acc = acc + [None] * 4
            for r, parts in enumerate(y_products(ylines, cell, group, lambda r: moved[cell * 4 + r, segs, :])):
                for s in range(9):
                    acc[r + s] = parts[s] if acc[r + s] is None else acc[r + s] + parts[s]
            for r in range(4):
                if cell < 3:
                    partial[4 * cell - 4 + r, segs, :] = acc[r]
                else:
                    finished(done, 4 * cell - 12 + r, group, acc[r])
            acc = acc[4:]
        for r in range(8):
            partial[8 + r, segs, :] = acc[r]


def edge_kernel(odd_ref, got, line_a, line_b, fine, rows_a, rows_b, partial, kept, matrix, done, rows_matrix, out, gx, gy, left_x, left_y, coefs, ylines, moved, edge, sems):
    inner_copy = pltpu.make_async_copy(done, out.at[pl.ds(GROUP, 4 * GROUP), :], sems.at[2])
    inner_copy.start()
    odd = odd_ref[0] == 1
    gx[8:16, :] = jnp.zeros((8, 768), jnp.float32)
    gy[8:16, :] = jnp.zeros((8, 768), jnp.float32)
    for i, j in enumerate(ORDER):
        at = slice(48 * j, 48 * j + 48)
        from_a, from_b = line_a[i], line_b[i]
        below, above = jnp.where(odd, from_a, from_b), jnp.where(odd, from_b, from_a)
        for row, values in ((0, below), (2, got[i, 0:2, :]), (4, got[i, 10:12, :]), (6, above)):
            gx[row : row + 2, at] = values[:, 0:48]
            gy[row : row + 2, at] = values[:, 64:112]
    fine_fields(gx[...], gy[...], left_x, left_y, coefs, ylines, matrix, rows_matrix[48:64, :])
    lane = lanes()
    for i, y in enumerate(EDGE_ROWS):
        if y in KEPT:
            moved[i] = kept[KEPT.index(y)]
            continue
        if 0 <= y < 48:
            value = fine[y]
        else:
            from_a, from_b = rows_a[y % 4], rows_b[y % 4]
            value = jnp.where(odd, from_a, from_b) if y < 0 else jnp.where(odd, from_b, from_a)
        moved[i] = x_swept(coefs, i, value, lane)

    for side, first in ((0, -1), (1, 11)):
        for group in range(3):
            segs = slice(TILE * group, TILE * group + TILE)
            acc = {40 * side + r: partial[8 * side + r, segs, :] for r in range(8)}
            for k in range(2):
                c, at = first + k, 8 * side + 4 * k
                for r, parts in enumerate(y_products(ylines, EDGE_CELLS.index(c), group, lambda r: moved[at + r, segs, :])):
                    for s, part in enumerate(parts):
                        row = 4 * c + r + s - 4
                        if row in acc:
                            acc[row] = acc[row] + part
            for r in range(8):
                finished(edge, 8 * side + r, group, acc[40 * side + r])
    copies = []
    for side, tile in ((0, 0), (1, 5)):
        copies.append(
            pltpu.make_async_copy(
                edge.at[pl.ds(side * GROUP, GROUP), :], out.at[pl.ds(tile * GROUP, GROUP), :], sems.at[side]
            )
        )
        copies[-1].start()
    for copy in [inner_copy] + copies:
        copy.wait()


def scratch(rows, ytiles):
    return [
        pltpu.VMEM((16, 768), jnp.float32),
        pltpu.VMEM((16, 768), jnp.float32),
        pltpu.VMEM((12 * rows, 256), jnp.bfloat16),
        pltpu.VMEM((12 * 16, 256), jnp.bfloat16),
        pltpu.VMEM((4, rows // TILE * SEGMENTS * PITCH, LANES), jnp.float32),
        pltpu.VMEM((ytiles * SEGMENTS * PITCH, LANES), jnp.float32),
        pltpu.VMEM((max(rows + 16, 48) if rows > 16 else rows, SEGMENTS, LANES), jnp.float32),
    ]


VMEM_SPEC = pl.BlockSpec(memory_space=pltpu.VMEM)
ANY_SPEC = pl.BlockSpec(memory_space=pl.ANY)
PARAMS = pltpu.CompilerParams(vmem_limit_bytes=32 * 2**20)


def rows_matrices():
    return jnp.asarray(
        np.concatenate([row_matrix(INNER_ROWS, INNER_CELLS), row_matrix(EDGE_ROWS, EDGE_CELLS)]), jnp.bfloat16
    )


def prepare(odd, scalar):
    rows = jax.ShapeDtypeStruct((4, SEGMENTS, LANES), jnp.float32)
    return pl.pallas_call(
        prepare_kernel,
        out_shape=(
            jax.ShapeDtypeStruct((48, SEGMENTS, LANES), jnp.float32),
            rows,
            rows,
            jax.ShapeDtypeStruct((256, 1024), jnp.bfloat16),
        ),
        in_specs=[pl.BlockSpec(memory_space=pltpu.SMEM), VMEM_SPEC],
        out_specs=(VMEM_SPEC,) * 4,
        compiler_params=PARAMS,
        name="prepare",
    )(odd, scalar)


def inner_sweeps(got, fine, matrix, rows_matrix):
    return pl.pallas_call(
        inner_kernel,
        out_shape=(
            jax.ShapeDtypeStruct((4 * GROUP, LANES), jnp.float32),
            jax.ShapeDtypeStruct((16, SEGMENTS, LANES), jnp.float32),
            jax.ShapeDtypeStruct((4, SEGMENTS, LANES), jnp.float32),
        ),
        in_specs=[VMEM_SPEC] * 4,
        out_specs=(VMEM_SPEC,) * 3,
        scratch_shapes=scratch(32, 2)
        + [
            pltpu.VMEM((12 * 16, 256), jnp.bfloat16),
            pltpu.VMEM((4, 2 * SEGMENTS * PITCH, LANES), jnp.float32),
        ],
        compiler_params=PARAMS,
        cost_estimate=pl.CostEstimate(flops=4 * 10**7, bytes_accessed=16 * 2**20, transcendentals=0),
        name="inner_sweeps",
    )(got, fine, matrix, rows_matrix)


def edge_sweeps(odd, got, line_a, line_b, fine, rows_a, rows_b, partial, kept, matrix, done, rows_matrix):
    return pl.pallas_call(
        edge_kernel,
        out_shape=jax.ShapeDtypeStruct((6 * GROUP, LANES), jnp.float32),
        in_specs=[pl.BlockSpec(memory_space=pltpu.SMEM)] + [VMEM_SPEC] * 11,
        out_specs=ANY_SPEC,
        scratch_shapes=scratch(16, 1)
        + [pltpu.VMEM((2 * GROUP, LANES), jnp.float32), pltpu.SemaphoreType.DMA((3,))],
        compiler_params=PARAMS,
        name="edge_sweeps",
    )(odd, got, line_a, line_b, fine, rows_a, rows_b, partial, kept, matrix, done, rows_matrix)


def local(scalar, x_velocity, y_velocity):
    count = lax.axis_size("row")
    pair_a = [(i, i ^ 1) for i in range(count)]
    pair_b = [(i, (i + (1 if i % 2 else -1)) % count) for i in range(count)]
    odd = lax.axis_index("row") % 2
    tiles = scalar.reshape(6, TILE, SEGMENTS, LANES).transpose(0, 2, 1, 3).reshape(6 * GROUP, LANES)
    parity = odd.astype(jnp.int32).reshape(1)
    got = lax.all_to_all(pack(x_velocity, y_velocity), "line", 0, 0, axis_index_groups=[ORDER], tiled=True)
    fine, send_a, send_b, matrix = prepare(parity, tiles)
    rows_a = lax.ppermute(send_a, "row", pair_a)
    rows_b = lax.ppermute(send_b, "row", pair_b)
    first, last = got[:, 0:2], got[:, 10:12]
    line_a = lax.ppermute(jnp.where(odd == 1, first, last), "row", pair_a)
    line_b = lax.ppermute(jnp.where(odd == 1, last, first), "row", pair_b)
    rows_matrix = rows_matrices()
    done, partial, kept = inner_sweeps(got, fine, matrix, rows_matrix)
    result = edge_sweeps(
        parity, got, line_a, line_b, fine, rows_a, rows_b, partial, kept, matrix, done, rows_matrix
    )
    return result.reshape(6, SEGMENTS, TILE, LANES).transpose(0, 2, 1, 3).reshape(1, 48, 3072)


def solution(mesh):
    in_specs = (P("line", "row", None), P(None, "row", "line"), P(None, "row", "line"))
    out_specs = P("line", "row", None)
    return jax.shard_map(local, mesh=mesh, in_specs=in_specs, out_specs=out_specs, check_vma=False)
```

```python
import functools

import jax
import jax.numpy as jnp
import numpy as np
from jax import lax
from jax.experimental import pallas as pl
from jax.experimental.pallas import tpu as pltpu
from jax.sharding import PartitionSpec as P

SEGMENTS, LANES, TILE = 24, 128, 8
GROUP = SEGMENTS * TILE
PITCH = 9
ORDER = [11, 15, 9, 13, 14, 10, 8, 12, 7, 5, 6, 4, 3, 1, 2, 0]


def kernel_parts():
    a = np.polynomial.Polynomial([0.0, 1.0])
    pieces = (
        (1.5, (a - 1) * (a - 2) * (25 * a**3 - 114 * a**2 + 153 * a - 48) / 24),
        (2.5, -(a - 2) * (a - 3) ** 3 * (5 * a - 8) / 24),
    )
    parts = []
    for middle, piece in pieces:
        coefs = piece(middle - a).coef
        for part in (coefs[0::2], coefs[1::2]):
            quotient, rest = divmod(np.polynomial.Polynomial(part), np.polynomial.Polynomial([-0.25, 1.0]))
            assert np.abs(rest.coef).max() < 1e-12
            parts.append([float(c) for c in quotient.coef])
    return parts


PARTS = kernel_parts()


def products(value, d):
    high = d >= 0.0
    size = jnp.abs(d)
    right = size >= 1.0
    t = jnp.abs(size - 1.0) - 0.5
    tau = t * t
    common = value * (tau - 0.25)
    common_t = common * t
    even1, odd1, even2, odd2 = (
        base * (line[1] * tau + line[0]) for base, line in zip((common, common_t) * 2, PARTS)
    )
    even0 = 0.5 * value - (even1 + even2)
    odd0 = value * t - (3.0 * odd1 + 5.0 * odd2)
    far0 = even0 - odd0
    near0 = even0 + odd0
    near1, far1 = even1 + odd1, even1 - odd1
    near2, far2 = even2 + odd2, even2 - odd2
    w = {
        1: far0,
        2: jnp.where(right, near0, far1),
        0: jnp.where(right, far1, near0),
        3: jnp.where(right, near1, far2),
        -1: jnp.where(right, far2, near1),
        4: jnp.where(right, near2, 0.0),
        -2: jnp.where(right, 0.0, near2),
    }
    return [w[0] if s == 0 else jnp.where(high, w.get(s, 0.0), w.get(-s, 0.0)) for s in range(-4, 5)]


def fill_matrix(out):
    row = lax.broadcasted_iota(jnp.int32, (128, 256), 0)
    fine = lax.broadcasted_iota(jnp.int32, (128, 256), 1)
    offset = row - 32 - (fine >> 2)
    v = ((fine & 3).astype(jnp.float32) - 1.5) * 0.25
    size = jnp.abs(v)
    own = jnp.where(offset == 0, 1.0, 0.0)
    next_cell = jnp.where(offset == 1, 1.0, 0.0)
    last_cell = jnp.where(offset == -1, 1.0, 0.0)
    value = own * (1.0 - size) + jnp.where(v > 0, next_cell, last_cell) * size
    low = 0.5 * value
    blocks = (jnp.where(row == 0, v, low), value + own, next_cell - own, own - last_cell)
    for q, block in enumerate(blocks):
        block = block.astype(jnp.bfloat16)
        out[0:128, 256 * q : 256 * q + 256] = block
        out[128:256, 256 * q : 256 * q + 256] = block if q else low.astype(jnp.bfloat16)


def row_matrix(fine_rows, coarse_rows):
    a = np.zeros((len(fine_rows), len(coarse_rows)))
    for i, y in enumerate(fine_rows):
        c, v = y // 4, (y % 4 - 1.5) / 4
        for cell, weight in ((c, 1 - abs(v)), (c + (1 if v > 0 else -1), abs(v))):
            if cell in coarse_rows:
                a[i, coarse_rows.index(cell)] += weight
    return np.concatenate([a, a], axis=1)


INNER_ROWS, INNER_CELLS = list(range(48)), list(range(12)) + [None] * 4
EDGE_ROWS = list(range(-4, 4)) + list(range(44, 52))
EDGE_CELLS = [-2, -1, 0, 1, 10, 11, 12, 13] + [None] * 8


def pack_kernel(x_ref, y_ref, out_ref, both):
    both[...] = jnp.zeros_like(both)
    both[:, :, 0:48] = x_ref[...]
    both[:, :, 64:112] = y_ref[...]
    for i, k in enumerate(ORDER):
        q, w = (k + 2) // 4, ((k + 2) % 4 + 0.5) / 4
        out_ref[i] = (1 - w) * both[q] + w * both[q + 1]


def pack(x, y):
    return pl.pallas_call(
        pack_kernel,
        out_shape=jax.ShapeDtypeStruct((16, 12, 128), jnp.float32),
        scratch_shapes=[pltpu.VMEM((6, 12, 128), jnp.float32)],
        name="pack_planes",
    )(x, y)


def split(values):
    high = values.astype(jnp.bfloat16)
    low = (values - high.astype(jnp.float32)).astype(jnp.bfloat16)
    return high, low


def windows(lines, lefts, first):
    rows = lines.shape[0]
    lane0 = lax.broadcasted_iota(jnp.int32, (rows, 128), 1) == 0
    rolled = [pltpu.roll(lines, shift, 1) for shift in (32, 96)]
    for m in range(12):
        at = (64 * m - 32 + (32, 96)[m % 2]) % 768
        high, low = split(jnp.where(lane0, first, rolled[m % 2][:, at : at + 128]))
        row = 0
        for left in lefts:
            count = left.shape[0] // 12
            for columns, part in ((slice(0, 128), high), (slice(128, 256), low)):
                left[m * count : (m + 1) * count, columns] = part[row : row + count]
            row += count


def spread(left, matrix, columns, rows, store):
    res = jnp.dot(left, matrix[:, columns], preferred_element_type=jnp.float32)
    for m in range(12):
        for h in range(2):
            for t in range(rows // TILE):
                at = m * rows + t * TILE
                store(t, 2 * m + h, res[at : at + TILE, LANES * h : LANES * h + LANES])


def x_lines(gx, rows_matrix):
    high, low = split(gx)
    lines = jnp.dot(rows_matrix[...], jnp.concatenate([high, low], axis=0), preferred_element_type=jnp.float32)
    return 0.8 * lines


def field(left, matrix, q, out):
    def store(t, seg, values):
        if t < out.shape[0] // (SEGMENTS * PITCH):
            out[pl.ds((t * SEGMENTS + seg) * PITCH, TILE), :] = values

    spread(left[...], matrix, slice(256 * q, 256 * q + 256), left.shape[0] // 12, store)


def fine_fields(gx, gy, left_x, left_y, coefs, ylines, matrix, rows_matrix):
    windows(x_lines(gx, rows_matrix), (left_x,), 1.0)
    windows(1.6 * gy, (left_y,), 0.0)
    for q in range(4):
        field(left_x, matrix, q, coefs.at[q])
    field(left_y, matrix, 0, ylines)


def row_at(row):
    return pl.ds((row // TILE) * GROUP + row % TILE, SEGMENTS, stride=TILE)


def field_at(row):
    return pl.ds((row // TILE) * (SEGMENTS * PITCH) + row % TILE, SEGMENTS, stride=PITCH)


def x_swept(coefs, row, value, lane):
    at = field_at(row)
    v, s, dp, dm = (coefs[q, at, :] for q in range(4))
    parts = products(value, s + v * jnp.where(v >= 0.0, dp, dm))
    total, wrap = parts[4], None
    for s in range(1, 5):
        raised = pltpu.roll(parts[4 + s], s, 1)
        lowered = pltpu.roll(parts[4 - s], LANES - s, 1)
        over = jnp.where(lane < s, raised, jnp.where(lane >= LANES - s, lowered, 0.0))
        wrap = over if wrap is None else wrap + over
        total = total + (raised + lowered)
    moved_wrap = jnp.where(lane < LANES // 2, pltpu.roll(wrap, 1, 0), pltpu.roll(wrap, SEGMENTS - 1, 0))
    return (total - wrap) + moved_wrap


def group_at(start, group, pitch):
    return pl.ds(start + group * TILE * pitch, TILE, stride=pitch)


def y_products(ylines, cell, group, source):
    at = (group_at((k // TILE) * (SEGMENTS * PITCH) + k % TILE, group, PITCH) for k in (cell - 1, cell, cell + 1))
    below, here, above = (ylines[rows, :] for rows in at)
    dm, dp = here - below, above - here
    for r in range(4):
        v0 = (r - 1.5) / 4
        u0 = here + v0 * (dp if v0 > 0 else dm)
        v = v0 + 0.5 * u0
        yield products(source(r), (u0 + here) + v * jnp.where(v >= 0.0, dp, dm))


def finished(ref, row, group, values):
    ref[group_at((row // TILE) * GROUP + row % TILE, group, TILE), :] = values


def lanes():
    return lax.broadcasted_iota(jnp.int32, (SEGMENTS, LANES), 1)


KEPT = (2, 3, 44, 45)


def prepare_kernel(odd_ref, scalar, fine, send_a, send_b, matrix):
    odd = odd_ref[0] == 1
    for y in range(48):
        fine[y] = scalar[row_at(y), :]
    for i in range(4):
        first, last = fine[i], fine[44 + i]
        send_a[i] = jnp.where(odd, first, last)
        send_b[i] = jnp.where(odd, last, first)
    fill_matrix(matrix)


def inner_kernel(got, fine, matrix, rows_matrix, done, partial, kept, gx, gy, left_x, left_y, coefs, ylines, moved, left_first, coefs_first):
    gx[8:16, :] = jnp.zeros((8, 768), jnp.float32)
    gy[8:16, :] = jnp.zeros((8, 768), jnp.float32)
    for i, j in enumerate(ORDER):
        gx[0:12, 48 * j : 48 * j + 48] = got[i, :, 0:48]
        gy[0:12, 48 * j : 48 * j + 48] = got[i, :, 64:112]
    windows(x_lines(gx[...], rows_matrix[0:48, :]), (left_first, left_x), 1.0)
    for q in range(4):
        field(left_first, matrix, q, coefs_first.at[q])
    windows(1.6 * gy[...], (left_y,), 0.0)
    lane = lanes()
    for q in range(5):
        field(left_x if q < 4 else left_y, matrix, q % 4, coefs.at[q] if q < 4 else ylines)
        for row in range(2 + 3 * q, min(5 + 3 * q, 16)):
            moved[row] = x_swept(coefs_first, row, fine[row], lane)

    def x_rows(block, carry):
        for r in range(15):
            row = block * 15 + r
            moved[row + 16] = x_swept(coefs, row, fine[row + 16], lane)
        return carry

    lax.fori_loop(0, 2, x_rows, 0)
    for i, row in enumerate(KEPT):
        kept[i] = moved[row]

    for group in range(3):
        segs = slice(TILE * group, TILE * group + TILE)
        acc = [None] * 8
        for cell in range(1, 11):
            acc = acc + [None] * 4
            for r, parts in enumerate(y_products(ylines, cell, group, lambda r: moved[cell * 4 + r, segs, :])):
                for s in range(9):
                    acc[r + s] = parts[s] if acc[r + s] is None else acc[r + s] + parts[s]
            for r in range(4):
                if cell < 3:
                    partial[4 * cell - 4 + r, segs, :] = acc[r]
                else:
                    finished(done, 4 * cell - 12 + r, group, acc[r])
            acc = acc[4:]
        for r in range(8):
            partial[8 + r, segs, :] = acc[r]


def edge_kernel(odd_ref, got, line_a, line_b, fine, rows_a, rows_b, partial, kept, matrix, done, rows_matrix, out, gx, gy, left_x, left_y, coefs, ylines, moved, edge, sems):
    inner_copy = pltpu.make_async_copy(done, out.at[pl.ds(GROUP, 4 * GROUP), :], sems.at[2])
    inner_copy.start()
    odd = odd_ref[0] == 1
    gx[8:16, :] = jnp.zeros((8, 768), jnp.float32)
    gy[8:16, :] = jnp.zeros((8, 768), jnp.float32)
    for i, j in enumerate(ORDER):
        at = slice(48 * j, 48 * j + 48)
        from_a, from_b = line_a[i], line_b[i]
        below, above = jnp.where(odd, from_a, from_b), jnp.where(odd, from_b, from_a)
        for row, values in ((0, below), (2, got[i, 0:2, :]), (4, got[i, 10:12, :]), (6, above)):
            gx[row : row + 2, at] = values[:, 0:48]
            gy[row : row + 2, at] = values[:, 64:112]
    fine_fields(gx[...], gy[...], left_x, left_y, coefs, ylines, matrix, rows_matrix[48:64, :])
    lane = lanes()
    for i, y in enumerate(EDGE_ROWS):
        if y in KEPT:
            moved[i] = kept[KEPT.index(y)]
            continue
        if 0 <= y < 48:
            value = fine[y]
        else:
            from_a, from_b = rows_a[y % 4], rows_b[y % 4]
            value = jnp.where(odd, from_a, from_b) if y < 0 else jnp.where(odd, from_b, from_a)
        moved[i] = x_swept(coefs, i, value, lane)

    for side, first in ((0, -1), (1, 11)):
        for group in range(3):
            segs = slice(TILE * group, TILE * group + TILE)
            acc = {40 * side + r: partial[8 * side + r, segs, :] for r in range(8)}
            for k in range(2):
                c, at = first + k, 8 * side + 4 * k
                for r, parts in enumerate(y_products(ylines, EDGE_CELLS.index(c), group, lambda r: moved[at + r, segs, :])):
                    for s, part in enumerate(parts):
                        row = 4 * c + r + s - 4
                        if row in acc:
                            acc[row] = acc[row] + part
            for r in range(8):
                finished(edge, 8 * side + r, group, acc[40 * side + r])
    copies = []
    for side, tile in ((0, 0), (1, 5)):
        copies.append(
            pltpu.make_async_copy(
                edge.at[pl.ds(side * GROUP, GROUP), :], out.at[pl.ds(tile * GROUP, GROUP), :], sems.at[side]
            )
        )
        copies[-1].start()
    for copy in [inner_copy] + copies:
        copy.wait()


def scratch(rows, ytiles):
    return [
        pltpu.VMEM((16, 768), jnp.float32),
        pltpu.VMEM((16, 768), jnp.float32),
        pltpu.VMEM((12 * rows, 256), jnp.bfloat16),
        pltpu.VMEM((12 * 16, 256), jnp.bfloat16),
        pltpu.VMEM((4, rows // TILE * SEGMENTS * PITCH, LANES), jnp.float32),
        pltpu.VMEM((ytiles * SEGMENTS * PITCH, LANES), jnp.float32),
        pltpu.VMEM((max(rows + 16, 48) if rows > 16 else rows, SEGMENTS, LANES), jnp.float32),
    ]


VMEM_SPEC = pl.BlockSpec(memory_space=pltpu.VMEM)
ANY_SPEC = pl.BlockSpec(memory_space=pl.ANY)
PARAMS = pltpu.CompilerParams(vmem_limit_bytes=32 * 2**20)


def rows_matrices():
    return jnp.asarray(
        np.concatenate([row_matrix(INNER_ROWS, INNER_CELLS), row_matrix(EDGE_ROWS, EDGE_CELLS)]), jnp.bfloat16
    )


def prepare(odd, scalar):
    rows = jax.ShapeDtypeStruct((4, SEGMENTS, LANES), jnp.float32)
    return pl.pallas_call(
        prepare_kernel,
        out_shape=(
            jax.ShapeDtypeStruct((48, SEGMENTS, LANES), jnp.float32),
            rows,
            rows,
            jax.ShapeDtypeStruct((256, 1024), jnp.bfloat16),
        ),
        in_specs=[pl.BlockSpec(memory_space=pltpu.SMEM), VMEM_SPEC],
        out_specs=(VMEM_SPEC,) * 4,
        compiler_params=PARAMS,
        name="prepare",
    )(odd, scalar)


def inner_sweeps(got, fine, matrix, rows_matrix):
    return pl.pallas_call(
        inner_kernel,
        out_shape=(
            jax.ShapeDtypeStruct((4 * GROUP, LANES), jnp.float32),
            jax.ShapeDtypeStruct((16, SEGMENTS, LANES), jnp.float32),
            jax.ShapeDtypeStruct((4, SEGMENTS, LANES), jnp.float32),
        ),
        in_specs=[VMEM_SPEC] * 4,
        out_specs=(VMEM_SPEC,) * 3,
        scratch_shapes=scratch(32, 2)
        + [
            pltpu.VMEM((12 * 16, 256), jnp.bfloat16),
            pltpu.VMEM((4, 2 * SEGMENTS * PITCH, LANES), jnp.float32),
        ],
        compiler_params=PARAMS,
        cost_estimate=pl.CostEstimate(flops=4 * 10**7, bytes_accessed=16 * 2**20, transcendentals=0),
        name="inner_sweeps",
    )(got, fine, matrix, rows_matrix)


def edge_sweeps(odd, got, line_a, line_b, fine, rows_a, rows_b, partial, kept, matrix, done, rows_matrix):
    return pl.pallas_call(
        edge_kernel,
        out_shape=jax.ShapeDtypeStruct((6 * GROUP, LANES), jnp.float32),
        in_specs=[pl.BlockSpec(memory_space=pltpu.SMEM)] + [VMEM_SPEC] * 11,
        out_specs=ANY_SPEC,
        scratch_shapes=scratch(16, 1)
        + [pltpu.VMEM((2 * GROUP, LANES), jnp.float32), pltpu.SemaphoreType.DMA((3,))],
        compiler_params=PARAMS,
        name="edge_sweeps",
    )(odd, got, line_a, line_b, fine, rows_a, rows_b, partial, kept, matrix, done, rows_matrix)


def local(scalar, x_velocity, y_velocity):
    count = lax.axis_size("row")
    pair_a = [(i, i ^ 1) for i in range(count)]
    pair_b = [(i, (i + (1 if i % 2 else -1)) % count) for i in range(count)]
    odd = lax.axis_index("row") % 2
    tiles = scalar.reshape(6, TILE, SEGMENTS, LANES).transpose(0, 2, 1, 3).reshape(6 * GROUP, LANES)
    parity = odd.astype(jnp.int32).reshape(1)
    got = lax.all_to_all(pack(x_velocity, y_velocity), "line", 0, 0, axis_index_groups=[ORDER], tiled=True)
    fine, send_a, send_b, matrix = prepare(parity, tiles)
    rows_a = lax.ppermute(send_a, "row", pair_a)
    rows_b = lax.ppermute(send_b, "row", pair_b)
    first, last = got[:, 0:2], got[:, 10:12]
    line_a = lax.ppermute(jnp.where(odd == 1, first, last), "row", pair_a)
    line_b = lax.ppermute(jnp.where(odd == 1, last, first), "row", pair_b)
    rows_matrix = rows_matrices()
    done, partial, kept = inner_sweeps(got, fine, matrix, rows_matrix)
    result = edge_sweeps(
        parity, got, line_a, line_b, fine, rows_a, rows_b, partial, kept, matrix, done, rows_matrix
    )
    return result.reshape(6, SEGMENTS, TILE, LANES).transpose(0, 2, 1, 3).reshape(1, 48, 3072)


def solution(mesh):
    in_specs = (P("line", "row", None), P(None, "row", "line"), P(None, "row", "line"))
    out_specs = P("line", "row", None)
    return jax.shard_map(local, mesh=mesh, in_specs=in_specs, out_specs=out_specs, check_vma=False)
```

```python
import functools

import jax
import jax.numpy as jnp
import numpy as np
from jax import lax
from jax.experimental import pallas as pl
from jax.experimental.pallas import tpu as pltpu
from jax.sharding import PartitionSpec as P

SEGMENTS, LANES, TILE = 24, 128, 8
GROUP = SEGMENTS * TILE
PITCH = 9
ORDER = [11, 15, 9, 13, 10, 14, 8, 12, 7, 5, 6, 4, 3, 1, 2, 0]


def kernel_parts():
    a = np.polynomial.Polynomial([0.0, 1.0])
    pieces = (
        (1.5, (a - 1) * (a - 2) * (25 * a**3 - 114 * a**2 + 153 * a - 48) / 24),
        (2.5, -(a - 2) * (a - 3) ** 3 * (5 * a - 8) / 24),
    )
    parts = []
    for middle, piece in pieces:
        coefs = piece(middle - a).coef
        for part in (coefs[0::2], coefs[1::2]):
            quotient, rest = divmod(np.polynomial.Polynomial(part), np.polynomial.Polynomial([-0.25, 1.0]))
            assert np.abs(rest.coef).max() < 1e-12
            parts.append([float(c) for c in quotient.coef])
    return parts


PARTS = kernel_parts()


def products(value, d):
    high = d >= 0.0
    size = jnp.abs(d)
    right = size >= 1.0
    t = jnp.abs(size - 1.0) - 0.5
    tau = t * t
    common = value * (tau - 0.25)
    common_t = common * t
    even1, odd1, even2, odd2 = (
        base * (line[1] * tau + line[0]) for base, line in zip((common, common_t) * 2, PARTS)
    )
    even0 = 0.5 * value - (even1 + even2)
    odd0 = value * t - (3.0 * odd1 + 5.0 * odd2)
    far0 = even0 - odd0
    near0 = even0 + odd0
    near1, far1 = even1 + odd1, even1 - odd1
    near2, far2 = even2 + odd2, even2 - odd2
    w = {
        1: far0,
        2: jnp.where(right, near0, far1),
        0: jnp.where(right, far1, near0),
        3: jnp.where(right, near1, far2),
        -1: jnp.where(right, far2, near1),
        4: jnp.where(right, near2, 0.0),
        -2: jnp.where(right, 0.0, near2),
    }
    return [w[0] if s == 0 else jnp.where(high, w.get(s, 0.0), w.get(-s, 0.0)) for s in range(-4, 5)]


def fill_matrix(out):
    row = lax.broadcasted_iota(jnp.int32, (128, 256), 0)
    fine = lax.broadcasted_iota(jnp.int32, (128, 256), 1)
    offset = row - 32 - (fine >> 2)
    v = ((fine & 3).astype(jnp.float32) - 1.5) * 0.25
    size = jnp.abs(v)
    own = jnp.where(offset == 0, 1.0, 0.0)
    next_cell = jnp.where(offset == 1, 1.0, 0.0)
    last_cell = jnp.where(offset == -1, 1.0, 0.0)
    value = own * (1.0 - size) + jnp.where(v > 0, next_cell, last_cell) * size
    low = 0.5 * value
    blocks = (jnp.where(row == 0, v, low), value + own, next_cell - own, own - last_cell)
    for q, block in enumerate(blocks):
        block = block.astype(jnp.bfloat16)
        out[0:128, 256 * q : 256 * q + 256] = block
        out[128:256, 256 * q : 256 * q + 256] = block if q else low.astype(jnp.bfloat16)


def row_matrix(fine_rows, coarse_rows):
    a = np.zeros((len(fine_rows), len(coarse_rows)))
    for i, y in enumerate(fine_rows):
        c, v = y // 4, (y % 4 - 1.5) / 4
        for cell, weight in ((c, 1 - abs(v)), (c + (1 if v > 0 else -1), abs(v))):
            if cell in coarse_rows:
                a[i, coarse_rows.index(cell)] += weight
    return np.concatenate([a, a], axis=1)


INNER_ROWS, INNER_CELLS = list(range(48)), list(range(12)) + [None] * 4
EDGE_ROWS = list(range(-4, 4)) + list(range(44, 52))
EDGE_CELLS = [-2, -1, 0, 1, 10, 11, 12, 13] + [None] * 8


def pack_kernel(x_ref, y_ref, out_ref, both):
    both[...] = jnp.zeros_like(both)
    both[:, :, 0:48] = x_ref[...]
    both[:, :, 64:112] = y_ref[...]
    for i, k in enumerate(ORDER):
        q, w = (k + 2) // 4, ((k + 2) % 4 + 0.5) / 4
        out_ref[i] = (1 - w) * both[q] + w * both[q + 1]


def pack(x, y):
    return pl.pallas_call(
        pack_kernel,
        out_shape=jax.ShapeDtypeStruct((16, 12, 128), jnp.float32),
        scratch_shapes=[pltpu.VMEM((6, 12, 128), jnp.float32)],
        name="pack_planes",
    )(x, y)


def split(values):
    high = values.astype(jnp.bfloat16)
    low = (values - high.astype(jnp.float32)).astype(jnp.bfloat16)
    return high, low


def windows(lines, lefts, first):
    rows = lines.shape[0]
    lane0 = lax.broadcasted_iota(jnp.int32, (rows, 128), 1) == 0
    rolled = [pltpu.roll(lines, shift, 1) for shift in (32, 96)]
    for m in range(12):
        at = (64 * m - 32 + (32, 96)[m % 2]) % 768
        high, low = split(jnp.where(lane0, first, rolled[m % 2][:, at : at + 128]))
        row = 0
        for left in lefts:
            count = left.shape[0] // 12
            for columns, part in ((slice(0, 128), high), (slice(128, 256), low)):
                left[m * count : (m + 1) * count, columns] = part[row : row + count]
            row += count


def spread(left, matrix, columns, rows, store):
    res = jnp.dot(left, matrix[:, columns], preferred_element_type=jnp.float32)
    for m in range(12):
        for h in range(2):
            for t in range(rows // TILE):
                at = m * rows + t * TILE
                store(t, 2 * m + h, res[at : at + TILE, LANES * h : LANES * h + LANES])


def x_lines(gx, rows_matrix):
    high, low = split(gx)
    lines = jnp.dot(rows_matrix[...], jnp.concatenate([high, low], axis=0), preferred_element_type=jnp.float32)
    return 0.8 * lines


def field(left, matrix, q, out):
    def store(t, seg, values):
        if t < out.shape[0] // (SEGMENTS * PITCH):
            out[pl.ds((t * SEGMENTS + seg) * PITCH, TILE), :] = values

    spread(left[...], matrix, slice(256 * q, 256 * q + 256), left.shape[0] // 12, store)


def fine_fields(gx, gy, left_x, left_y, coefs, ylines, matrix, rows_matrix):
    windows(x_lines(gx, rows_matrix), (left_x,), 1.0)
    windows(1.6 * gy, (left_y,), 0.0)
    for q in range(4):
        field(left_x, matrix, q, coefs.at[q])
    field(left_y, matrix, 0, ylines)


def row_at(row):
    return pl.ds((row // TILE) * GROUP + row % TILE, SEGMENTS, stride=TILE)


def field_at(row):
    return pl.ds((row // TILE) * (SEGMENTS * PITCH) + row % TILE, SEGMENTS, stride=PITCH)


def x_swept(coefs, row, value, lane):
    at = field_at(row)
    v, s, dp, dm = (coefs[q, at, :] for q in range(4))
    parts = products(value, s + v * jnp.where(v >= 0.0, dp, dm))
    total, wrap = parts[4], None
    for s in range(1, 5):
        raised = pltpu.roll(parts[4 + s], s, 1)
        lowered = pltpu.roll(parts[4 - s], LANES - s, 1)
        over = jnp.where(lane < s, raised, jnp.where(lane >= LANES - s, lowered, 0.0))
        wrap = over if wrap is None else wrap + over
        total = total + (raised + lowered)
    moved_wrap = jnp.where(lane < LANES // 2, pltpu.roll(wrap, 1, 0), pltpu.roll(wrap, SEGMENTS - 1, 0))
    return (total - wrap) + moved_wrap


def group_at(start, group, pitch):
    return pl.ds(start + group * TILE * pitch, TILE, stride=pitch)


def y_products(ylines, cell, group, source):
    at = (group_at((k // TILE) * (SEGMENTS * PITCH) + k % TILE, group, PITCH) for k in (cell - 1, cell, cell + 1))
    below, here, above = (ylines[rows, :] for rows in at)
    dm, dp = here - below, above - here
    for r in range(4):
        v0 = (r - 1.5) / 4
        u0 = here + v0 * (dp if v0 > 0 else dm)
        v = v0 + 0.5 * u0
        yield products(source(r), (u0 + here) + v * jnp.where(v >= 0.0, dp, dm))


def finished(ref, row, group, values):
    ref[group_at((row // TILE) * GROUP + row % TILE, group, TILE), :] = values


def lanes():
    return lax.broadcasted_iota(jnp.int32, (SEGMENTS, LANES), 1)


KEPT = (2, 3, 44, 45)


def prepare_kernel(odd_ref, tiles, fine, send_a, send_b, matrix, scalar, sem):
    load = pltpu.make_async_copy(tiles, scalar, sem)
    load.start()
    fill_matrix(matrix)
    odd = odd_ref[0] == 1
    load.wait()
    for y in range(48):
        fine[y] = scalar[row_at(y), :]
    for i in range(4):
        first, last = fine[i], fine[44 + i]
        send_a[i] = jnp.where(odd, first, last)
        send_b[i] = jnp.where(odd, last, first)


def inner_kernel(got, fine, matrix, rows_matrix, done, partial, kept, gx, gy, left_x, left_y, coefs, ylines, moved, left_first, coefs_first):
    gx[8:16, :] = jnp.zeros((8, 768), jnp.float32)
    gy[8:16, :] = jnp.zeros((8, 768), jnp.float32)
    for i, j in enumerate(ORDER):
        gx[0:12, 48 * j : 48 * j + 48] = got[i, :, 0:48]
        gy[0:12, 48 * j : 48 * j + 48] = got[i, :, 64:112]
    windows(x_lines(gx[...], rows_matrix[0:48, :]), (left_first, left_x), 1.0)
    for q in range(4):
        field(left_first, matrix, q, coefs_first.at[q])
    windows(1.6 * gy[...], (left_y,), 0.0)
    lane = lanes()
    for q in range(5):
        field(left_x if q < 4 else left_y, matrix, q % 4, coefs.at[q] if q < 4 else ylines)
        for row in range(2 + 3 * q, min(5 + 3 * q, 16)):
            moved[row] = x_swept(coefs_first, row, fine[row], lane)

    def x_rows(block, carry):
        for r in range(15):
            row = block * 15 + r
            moved[row + 16] = x_swept(coefs, row, fine[row + 16], lane)
        return carry

    lax.fori_loop(0, 2, x_rows, 0)
    for i, row in enumerate(KEPT):
        kept[i] = moved[row]

    for group in range(3):
        segs = slice(TILE * group, TILE * group + TILE)
        acc = [None] * 8
        for cell in range(1, 11):
            acc = acc + [None] * 4
            for r, parts in enumerate(y_products(ylines, cell, group, lambda r: moved[cell * 4 + r, segs, :])):
                for s in range(9):
                    acc[r + s] = parts[s] if acc[r + s] is None else acc[r + s] + parts[s]
            for r in range(4):
                if cell < 3:
                    partial[4 * cell - 4 + r, segs, :] = acc[r]
                else:
                    finished(done, 4 * cell - 12 + r, group, acc[r])
            acc = acc[4:]
        for r in range(8):
            partial[8 + r, segs, :] = acc[r]


def edge_kernel(odd_ref, got, line_a, line_b, fine, rows_a, rows_b, partial, kept, matrix, done, rows_matrix, out, gx, gy, left_x, left_y, coefs, ylines, moved, edge, sems):
    inner_copy = pltpu.make_async_copy(done, out.at[pl.ds(GROUP, 4 * GROUP), :], sems.at[2])
    inner_copy.start()
    odd = odd_ref[0] == 1
    gx[8:16, :] = jnp.zeros((8, 768), jnp.float32)
    gy[8:16, :] = jnp.zeros((8, 768), jnp.float32)
    for i, j in enumerate(ORDER):
        at = slice(48 * j, 48 * j + 48)
        from_a, from_b = line_a[i], line_b[i]
        below, above = jnp.where(odd, from_a, from_b), jnp.where(odd, from_b, from_a)
        for row, values in ((0, below), (2, got[i, 0:2, :]), (4, got[i, 10:12, :]), (6, above)):
            gx[row : row + 2, at] = values[:, 0:48]
            gy[row : row + 2, at] = values[:, 64:112]
    fine_fields(gx[...], gy[...], left_x, left_y, coefs, ylines, matrix, rows_matrix[48:64, :])
    lane = lanes()
    for i, y in enumerate(EDGE_ROWS):
        if y in KEPT:
            moved[i] = kept[KEPT.index(y)]
            continue
        if 0 <= y < 48:
            value = fine[y]
        else:
            from_a, from_b = rows_a[y % 4], rows_b[y % 4]
            value = jnp.where(odd, from_a, from_b) if y < 0 else jnp.where(odd, from_b, from_a)
        moved[i] = x_swept(coefs, i, value, lane)

    for side, first in ((0, -1), (1, 11)):
        for group in range(3):
            segs = slice(TILE * group, TILE * group + TILE)
            acc = {40 * side + r: partial[8 * side + r, segs, :] for r in range(8)}
            for k in range(2):
                c, at = first + k, 8 * side + 4 * k
                for r, parts in enumerate(y_products(ylines, EDGE_CELLS.index(c), group, lambda r: moved[at + r, segs, :])):
                    for s, part in enumerate(parts):
                        row = 4 * c + r + s - 4
                        if row in acc:
                            acc[row] = acc[row] + part
            for r in range(8):
                finished(edge, 8 * side + r, group, acc[40 * side + r])
    copies = []
    for side, tile in ((0, 0), (1, 5)):
        copies.append(
            pltpu.make_async_copy(
                edge.at[pl.ds(side * GROUP, GROUP), :], out.at[pl.ds(tile * GROUP, GROUP), :], sems.at[side]
            )
        )
        copies[-1].start()
    for copy in [inner_copy] + copies:
        copy.wait()


def scratch(rows, ytiles):
    return [
        pltpu.VMEM((16, 768), jnp.float32),
        pltpu.VMEM((16, 768), jnp.float32),
        pltpu.VMEM((12 * rows, 256), jnp.bfloat16),
        pltpu.VMEM((12 * 16, 256), jnp.bfloat16),
        pltpu.VMEM((4, rows // TILE * SEGMENTS * PITCH, LANES), jnp.float32),
        pltpu.VMEM((ytiles * SEGMENTS * PITCH, LANES), jnp.float32),
        pltpu.VMEM((max(rows + 16, 48) if rows > 16 else rows, SEGMENTS, LANES), jnp.float32),
    ]


VMEM_SPEC = pl.BlockSpec(memory_space=pltpu.VMEM)
ANY_SPEC = pl.BlockSpec(memory_space=pl.ANY)
PARAMS = pltpu.CompilerParams(vmem_limit_bytes=32 * 2**20)


def rows_matrices():
    return jnp.asarray(
        np.concatenate([row_matrix(INNER_ROWS, INNER_CELLS), row_matrix(EDGE_ROWS, EDGE_CELLS)]), jnp.bfloat16
    )


def prepare(odd, scalar):
    rows = jax.ShapeDtypeStruct((4, SEGMENTS, LANES), jnp.float32)
    return pl.pallas_call(
        prepare_kernel,
        out_shape=(
            jax.ShapeDtypeStruct((48, SEGMENTS, LANES), jnp.float32),
            rows,
            rows,
            jax.ShapeDtypeStruct((256, 1024), jnp.bfloat16),
        ),
        in_specs=[pl.BlockSpec(memory_space=pltpu.SMEM), ANY_SPEC],
        out_specs=(VMEM_SPEC,) * 4,
        scratch_shapes=[pltpu.VMEM((6 * GROUP, LANES), jnp.float32), pltpu.SemaphoreType.DMA],
        compiler_params=PARAMS,
        name="prepare",
    )(odd, scalar)


def inner_sweeps(got, fine, matrix, rows_matrix):
    return pl.pallas_call(
        inner_kernel,
        out_shape=(
            jax.ShapeDtypeStruct((4 * GROUP, LANES), jnp.float32),
            jax.ShapeDtypeStruct((16, SEGMENTS, LANES), jnp.float32),
            jax.ShapeDtypeStruct((4, SEGMENTS, LANES), jnp.float32),
        ),
        in_specs=[VMEM_SPEC] * 4,
        out_specs=(VMEM_SPEC,) * 3,
        scratch_shapes=scratch(32, 2)
        + [
            pltpu.VMEM((12 * 16, 256), jnp.bfloat16),
            pltpu.VMEM((4, 2 * SEGMENTS * PITCH, LANES), jnp.float32),
        ],
        compiler_params=PARAMS,
        cost_estimate=pl.CostEstimate(flops=4 * 10**7, bytes_accessed=16 * 2**20, transcendentals=0),
        name="inner_sweeps",
    )(got, fine, matrix, rows_matrix)


def edge_sweeps(odd, got, line_a, line_b, fine, rows_a, rows_b, partial, kept, matrix, done, rows_matrix):
    return pl.pallas_call(
        edge_kernel,
        out_shape=jax.ShapeDtypeStruct((6 * GROUP, LANES), jnp.float32),
        in_specs=[pl.BlockSpec(memory_space=pltpu.SMEM)] + [VMEM_SPEC] * 11,
        out_specs=ANY_SPEC,
        scratch_shapes=scratch(16, 1)
        + [pltpu.VMEM((2 * GROUP, LANES), jnp.float32), pltpu.SemaphoreType.DMA((3,))],
        compiler_params=PARAMS,
        name="edge_sweeps",
    )(odd, got, line_a, line_b, fine, rows_a, rows_b, partial, kept, matrix, done, rows_matrix)


def local(scalar, x_velocity, y_velocity):
    count = lax.axis_size("row")
    pair_a = [(i, i ^ 1) for i in range(count)]
    pair_b = [(i, (i + (1 if i % 2 else -1)) % count) for i in range(count)]
    odd = lax.axis_index("row") % 2
    tiles = scalar.reshape(6, TILE, SEGMENTS, LANES).transpose(0, 2, 1, 3).reshape(6 * GROUP, LANES)
    parity = odd.astype(jnp.int32).reshape(1)
    got = lax.all_to_all(pack(x_velocity, y_velocity), "line", 0, 0, axis_index_groups=[ORDER], tiled=True)
    fine, send_a, send_b, matrix = prepare(parity, tiles)
    rows_a = lax.ppermute(send_a, "row", pair_a)
    rows_b = lax.ppermute(send_b, "row", pair_b)
    first, last = got[:, 0:2], got[:, 10:12]
    line_a = lax.ppermute(jnp.where(odd == 1, first, last), "row", pair_a)
    line_b = lax.ppermute(jnp.where(odd == 1, last, first), "row", pair_b)
    rows_matrix = rows_matrices()
    done, partial, kept = inner_sweeps(got, fine, matrix, rows_matrix)
    result = edge_sweeps(
        parity, got, line_a, line_b, fine, rows_a, rows_b, partial, kept, matrix, done, rows_matrix
    )
    return result.reshape(6, SEGMENTS, TILE, LANES).transpose(0, 2, 1, 3).reshape(1, 48, 3072)


def solution(mesh):
    in_specs = (P("line", "row", None), P(None, "row", "line"), P(None, "row", "line"))
    out_specs = P("line", "row", None)
    return jax.shard_map(local, mesh=mesh, in_specs=in_specs, out_specs=out_specs, check_vma=False)
```
